128 devices in a mesh: gx: 8 (over y, core), gy: 16 (over x, z).
Axes of the slice: x: 4, y: 4, z: 4, core: 2. Of those that a mesh axis runs over, the one named last changes fastest.
Arguments:
- points: bfloat16 [524288, 128], P(('gx', 'gy')), may hold values from -6 to 6
- occupied: int32 [524288], P(('gx', 'gy')), may hold values 0 or 1
- z_order: int32 [128, 4096], P(('gx', 'gy')), may hold values from 0 to 4095, each once within a row
- pad_mask: int32 [128, 4096], P(('gx', 'gy')), may hold values 0 or 1
- hilbert_order: int32 [128, 4096], P(('gx', 'gy')), may hold values from 0 to 4095, each once within a row
- send_counts: int32 [128, 128], P(('gx', 'gy')), may hold values from 0 to 40, as said below
- w_conv: bfloat16 [27, 128, 128], replicated, may hold values from -0.109375 to 0.109375
- cpe_proj: bfloat16 [128, 128], replicated, may hold values from -0.5 to 0.5
- cpe_gain: float32 [128], replicated, may hold values from 0.5 to 1.5
- attn_gain: float32 [128], replicated, may hold values from 0.5 to 1.5
- w_qkv: bfloat16 [128, 384], replicated, may hold values from -4 to 4
- w_out: bfloat16 [128, 128], replicated, may hold values from -0.5 to 0.5
- mlp_gain: float32 [128], replicated, may hold values from 0.5 to 1.5
- w_up: bfloat16 [128, 512], replicated, may hold values from -0.5 to 0.5
- w_down: bfloat16 [512, 128], replicated, may hold values from -0.25 to 0.25
Outputs:
- moved: bfloat16 [655360, 128], P(('gx', 'gy'))
The draws below stay inside these ranges and needn't reach their ends.
Inputs may be any that keep to these rules, and one draw needn't show every extreme that they name: `send_counts`: each row sums to 4096; one new owner receives exactly 40 rows from every tile.
All inputs are finite; a program needn't handle non-finite values. No bound on the sum of `occupied` or of `pad_mask` on one device may be relied on, other than what follows from the above.
Results may differ from the reference program's by a relative error of at most 0.012.
The reference program's roundings to bfloat16 on the way count: a program that leaves them out, or rounds other values in their place, can miss the bound.
Values may be sent and summed in bfloat16 or wider, within the bound.
A program may use at most 64 MiB of HBM per device.

```python
import math
import jax
import jax.numpy as jnp
from jax import lax

C = 128
HEADS = 8
FF = 512
PATCH = 1024
TAPS = 27
LA = 16
LB = 16
POINTS_DEV = 4096
LZ = 16
HEAD_DIM = 16
TOKENS = 524288
CAP = 40
N_GX = 8
N_GY = 16
DEVICES = 128


def draw_w_qkv(key, part):
    key = jax.random.fold_in(key, 5)
    key_shared, key_distinct, key_value = jax.random.split(key, 3)
    spread = 1.0 / math.sqrt(C)
    shared = jax.random.normal(key_shared, (C, C), jnp.float32) * spread
    distinct = jax.random.normal(key_distinct, (C, C), jnp.float32) * spread
    values = jax.random.normal(key_value, (C, C), jnp.float32) * spread
    queries = shared
    keyed = distinct
    joined = jnp.concatenate([queries, keyed, values], axis=1)
    return jnp.clip(joined, -4.0, 4.0).astype(jnp.bfloat16)


def draw_send_counts(key, part):
    key = jax.random.fold_in(key, 9)
    key_owner, key_perm, key_pair = jax.random.split(key, 3)
    owner_id = jax.random.randint(key_owner, (), 0, DEVICES)
    others = DEVICES - 1
    remain = POINTS_DEV - CAP
    base_count = remain // others
    extra_rows = remain % others
    margin = max(0, min(base_count, CAP - 1 - base_count))
    rank_ids = jnp.arange(others, dtype=jnp.int32)
    levels = base_count + (rank_ids < extra_rows).astype(jnp.int32)
    pair_count = others // 2
    offset = jax.random.randint(key_pair, (DEVICES, pair_count), -margin, margin + 1)
    deltas = jnp.zeros((DEVICES, others), jnp.int32)
    deltas = deltas.at[:, 0:2 * pair_count:2].add(offset).at[:, 1:2 * pair_count:2].add(-offset)
    amounts = levels[None, :] + deltas
    orders = jax.vmap(lambda sub_key: jax.random.permutation(sub_key, others))(jax.random.split(key_perm, DEVICES))
    row_ids = jnp.arange(DEVICES, dtype=jnp.int32)[:, None]
    spread_counts = jnp.zeros((DEVICES, others), jnp.int32).at[row_ids, orders].set(amounts)
    target = jnp.arange(DEVICES, dtype=jnp.int32)
    source_col = jnp.clip(target - (target > owner_id).astype(jnp.int32), 0, others - 1)
    gathered = spread_counts[:, source_col]
    return jnp.where((target == owner_id)[None, :], CAP, gathered).astype(jnp.int32)


def set_ends(result, stream_key, low, high):
    extent = result.shape
    spot = [jax.random.randint(jax.random.fold_in(stream_key, axis), (), 0, extent[axis]) for axis in range(len(extent))]
    result = result.at[tuple(spot)].set(low)
    longest = extent.index(max(extent))
    spot[longest] = (spot[longest] + 1) % extent[longest]
    return result.at[tuple(spot)].set(high)


def level_of(key, dims, shards, smallest, high):
    def one(axis_at, shards_of):
        steps = jax.random.uniform(jax.random.fold_in(jax.random.fold_in(key, 6), axis_at), (shards_of,), jnp.float32, smallest / len(shards), high / len(shards))
        return jnp.repeat(jnp.exp(steps), dims[axis_at] // shards_of).reshape((-1,) + (1,) * (len(dims) - axis_at - 1))

    factor_of = one(*shards[0])
    for cut in shards[1:]:
        factor_of = factor_of * one(*cut)
    return factor_of


def scatter_about(key, shape, scale, bound, shards=(), kind=jnp.bfloat16):
    values = scale * jax.random.normal(key, shape, jnp.float32)
    if shards:
        values = values * level_of(key, shape, shards, -0.22, 0.18)
    return jnp.clip(values, -bound, bound).astype(kind)


def setup_inputs(seed: int = 0) -> dict:
    arg_keys = jax.random.split(jax.random.key(seed), 16)
    points = scatter_about(arg_keys[0], (TOKENS, C), 1.0, 6.0, ((0, 128),))
    occupied = set_ends((jax.random.randint(arg_keys[1], (TOKENS,), 0, 4) < 3).astype(jnp.int32), jax.random.fold_in(arg_keys[1], 1), 0, 1)
    z_order = jax.vmap(lambda own: jax.random.permutation(own, POINTS_DEV))(jax.random.split(arg_keys[2], DEVICES)).reshape((DEVICES, POINTS_DEV)).astype(jnp.int32)
    pad_mask = set_ends((jax.random.randint(arg_keys[3], (DEVICES, POINTS_DEV), 0, 8) < 7).astype(jnp.int32), jax.random.fold_in(arg_keys[3], 1), 0, 1)
    hilbert_order = jax.vmap(lambda own: jax.random.permutation(own, POINTS_DEV))(jax.random.split(arg_keys[4], DEVICES)).reshape((DEVICES, POINTS_DEV)).astype(jnp.int32)
    send_counts = draw_send_counts(jax.random.fold_in(arg_keys[15], 71), 0)
    w_conv = scatter_about(arg_keys[6], (TAPS, C, C), (TAPS * C) ** -0.5, 0.109375)
    cpe_proj = scatter_about(arg_keys[7], (C, C), C ** -0.5, 0.5)
    cpe_gain = jnp.clip(1.0 + 0.1 * jax.random.normal(arg_keys[8], (C,), jnp.float32), 0.5, 1.5)
    attn_gain = jnp.clip(1.0 + 0.1 * jax.random.normal(arg_keys[9], (C,), jnp.float32), 0.5, 1.5)
    w_qkv = draw_w_qkv(jax.random.fold_in(arg_keys[15], 71), 0)
    w_out = scatter_about(arg_keys[11], (C, C), C ** -0.5, 0.5)
    mlp_gain = jnp.clip(1.0 + 0.1 * jax.random.normal(arg_keys[12], (C,), jnp.float32), 0.5, 1.5)
    w_up = scatter_about(arg_keys[13], (C, FF), C ** -0.5, 0.5)
    w_down = scatter_about(arg_keys[14], (FF, C), FF ** -0.5, 0.25)
    return {"points": points, "occupied": occupied, "z_order": z_order, "pad_mask": pad_mask, "hilbert_order": hilbert_order, "send_counts": send_counts, "w_conv": w_conv, "cpe_proj": cpe_proj, "cpe_gain": cpe_gain, "attn_gain": attn_gain, "w_qkv": w_qkv, "w_out": w_out, "mlp_gain": mlp_gain, "w_up": w_up, "w_down": w_down}


def layer_norm(values, gain):
    center = values - lax.optimization_barrier(jnp.mean(values, axis=-1, keepdims=True))
    spread = lax.optimization_barrier(jnp.mean(center * center, axis=-1, keepdims=True))
    return center * lax.rsqrt(spread + 1e-05) * gain

def attend(block_items):
    queries, keys_in, values_in, alive_keys = block_items
    scores = jnp.einsum('hqd,hkd->hqk', queries.astype(jnp.float32), keys_in.astype(jnp.float32)) * HEAD_DIM ** (-0.5)
    length = scores.shape[-1]
    diagonal_mask = lax.broadcasted_iota(jnp.int32, (1, length, length), 1) == lax.broadcasted_iota(jnp.int32, (1, length, length), 2)
    allowed = (alive_keys[None, None, :] > 0) | diagonal_mask
    masked = jnp.where(allowed, scores, -1e+30)
    row_peak = lax.optimization_barrier(jnp.max(masked, axis=-1, keepdims=True))
    weights = jnp.where(allowed, jnp.exp(masked - row_peak), 0.0)
    attn_probs = (weights / lax.optimization_barrier(jnp.sum(weights, axis=-1, keepdims=True))).astype(jnp.bfloat16)
    mixed_heads = jnp.einsum('hqk,hkd->hqd', attn_probs.astype(jnp.float32), values_in.astype(jnp.float32))
    return mixed_heads.astype(jnp.bfloat16)

def split_heads(matrix, patch_count):
    shaped = matrix.reshape(patch_count, PATCH, HEADS // 2, 2, HEAD_DIM).transpose(0, 2, 3, 1, 4)
    return shaped.reshape(patch_count * (HEADS // 2), 2, PATCH, HEAD_DIM)

def join_heads(blocks, patch_count):
    shaped = blocks.reshape(patch_count, HEADS // 2, 2, PATCH, HEAD_DIM).transpose(0, 3, 1, 2, 4)
    return shaped.reshape(patch_count * PATCH, C)

def voxel_conv(window, w_conv):
    total = jnp.zeros((LA * LB * LZ, C), jnp.float32)
    for step_a in range(3):
        for step_b in range(3):
            for step_z in range(3):
                tap = step_a * 9 + step_b * 3 + step_z
                piece = window[step_a:step_a + LA, step_b:step_b + LB, step_z:step_z + LZ].reshape(LA * LB * LZ, C)
                total = total + jnp.dot(piece, w_conv[tap], preferred_element_type=jnp.float32)
    return total

def reference(points, occupied, z_order, pad_mask, hilbert_order, send_counts, w_conv, cpe_proj, cpe_gain, attn_gain, w_qkv, w_out, mlp_gain, w_up, w_down):
    filled = jnp.where(occupied[:, None] > 0, points, jnp.zeros_like(points))
    slab = filled.reshape(N_GX, N_GY, LA, LB, LZ, C).transpose(0, 2, 1, 3, 4, 5).reshape(N_GX * LA, N_GY * LB, LZ, C)
    padded = jnp.pad(slab, ((1, 1), (1, 1), (1, 1), (0, 0)))
    patch_count = POINTS_DEV // PATCH

    def one_device(device_items):
        device_id, local_points, order_row, alive_row, hilbert_row, count_row = device_items
        row_start = (device_id // N_GY * LA).astype(jnp.int32)
        col_start = (device_id % N_GY * LB).astype(jnp.int32)
        zero_start = jnp.zeros((), jnp.int32)
        window = lax.dynamic_slice(padded, (row_start, col_start, zero_start, zero_start), (LA + 2, LB + 2, LZ + 2, C))
        conv_out = voxel_conv(window, w_conv).astype(jnp.bfloat16)
        encoded = layer_norm(jnp.dot(conv_out, cpe_proj, preferred_element_type=jnp.float32), cpe_gain)
        residual = local_points.astype(jnp.float32) + encoded
        serial = jnp.take(residual, order_row, axis=0)
        attn_in = layer_norm(serial, attn_gain).astype(jnp.bfloat16)
        projected = jnp.dot(attn_in, w_qkv, preferred_element_type=jnp.float32).astype(jnp.bfloat16)
        queries = split_heads(projected[:, :C], patch_count)
        keys_in = split_heads(projected[:, C:2 * C], patch_count)
        values_in = split_heads(projected[:, 2 * C:], patch_count)
        alive_keys = jnp.broadcast_to(alive_row.reshape(patch_count, 1, PATCH), (patch_count, HEADS // 2, PATCH)).reshape(-1, PATCH)
        heads_out = join_heads(lax.map(attend, (queries, keys_in, values_in, alive_keys)), patch_count)
        attn_part = jnp.dot(heads_out, w_out, preferred_element_type=jnp.float32)
        mixed = serial + alive_row.astype(jnp.float32)[:, None] * attn_part
        mlp_in = layer_norm(mixed, mlp_gain).astype(jnp.bfloat16)
        hidden = jax.nn.gelu(jnp.dot(mlp_in, w_up, preferred_element_type=jnp.float32)).astype(jnp.bfloat16)
        block_out = (mixed + jnp.dot(hidden, w_down, preferred_element_type=jnp.float32)).astype(jnp.bfloat16)
        ordered = jnp.take(block_out, hilbert_row, axis=0)
        starts = (jnp.cumsum(count_row) - count_row).astype(jnp.int32)
        slot_ids = jnp.arange(CAP, dtype=jnp.int32)
        picks = starts[:, None] + slot_ids[None, :]
        valid = slot_ids[None, :] < count_row[:, None]
        rows_out = jnp.take(ordered, jnp.clip(picks, 0, POINTS_DEV - 1).reshape(-1).astype(jnp.int32), axis=0).reshape(DEVICES, CAP, C)
        return jnp.where(valid[:, :, None], rows_out, jnp.zeros_like(rows_out))
    device_ids = jnp.arange(DEVICES, dtype=jnp.int32)
    buffers = lax.map(one_device, (device_ids, points.reshape(DEVICES, POINTS_DEV, C), z_order, pad_mask, hilbert_order, send_counts))
    return buffers.transpose(1, 0, 2, 3).reshape(DEVICES * DEVICES * CAP, C)
```

```python
import functools
import jax
import jax.numpy as jnp
from jax import lax
from jax.experimental import pallas as pl
from jax.experimental.pallas import tpu as pltpu
from jax.sharding import PartitionSpec as P

C = 128
LA = 16
LB = 16
HEADS = 8
PATCH = 1024
HEAD_DIM = 16
QB = 256


def norm_rows(v, gain):
    center = v - jnp.mean(v, axis=-1, keepdims=True)
    spread = jnp.mean(center * center, axis=-1, keepdims=True)
    return center * lax.rsqrt(spread + 1e-05) * gain


def attn_kernel(zord, pad, res, gain, wqkv, wout, out, serial, qs, kt, va, heads, bd):
    rows = serial.shape[0]

    def gather(i, carry):
        base = i * 16
        for u in range(16):
            idx = zord[0, base + u]
            serial[pl.ds(base + u, 1), :] = res[pl.ds(idx, 1), :]
        return carry

    lax.fori_loop(0, rows // 16, gather, 0)

    va[:, C:] = jnp.ones((PATCH, C), jnp.bfloat16)
    sub = lax.broadcasted_iota(jnp.int32, (C, PATCH), 0)

    def patch(p, carry):
        off = pl.multiple_of(p * PATCH, PATCH)
        attn_in = norm_rows(serial[pl.ds(off, PATCH), :], gain[...]).astype(jnp.bfloat16)
        proj = jnp.dot(attn_in, wqkv[...], preferred_element_type=jnp.float32).astype(jnp.bfloat16)
        qs[...] = proj[:, :C] * jnp.bfloat16(HEAD_DIM ** -0.5)
        kt[:C, :] = proj[:, C : 2 * C].T
        va[:, :C] = proj[:, 2 * C :]
        bias = jnp.where(pad[:, pl.ds(off, PATCH)] > 0, 0.0, -1e30)
        kt[C:, :] = jnp.where(sub == 0, jnp.broadcast_to(bias, (C, PATCH)), 0.0).astype(jnp.bfloat16)
        rr = lax.broadcasted_iota(jnp.int32, (QB, QB), 0)
        cc = lax.broadcasted_iota(jnp.int32, (QB, QB), 1)
        for b in range(PATCH // QB):
            bd[b] = jnp.where(rr == cc, 0.0, bias[:, b * QB : (b + 1) * QB])

        def head(h, carry):
            lane = lax.broadcasted_iota(jnp.int32, (QB, C), 1)
            mine = lane // HEAD_DIM == h
            one = jnp.where(lane == 0, 1.0, 0.0).astype(jnp.bfloat16)
            for b in range(PATCH // QB):
                sl = slice(b * QB, (b + 1) * QB)
                q = jnp.where(mine, qs[sl, :], jnp.bfloat16(0))
                qa = jnp.concatenate([q, one], axis=1)
                parts = []
                for t in range(PATCH // QB):
                    ts = slice(t * QB, (t + 1) * QB)
                    if t == b:
                        parts.append(
                            jnp.dot(q, kt[:C, ts], preferred_element_type=jnp.float32) + bd[b]
                        )
                    else:
                        parts.append(jnp.dot(qa, kt[:, ts], preferred_element_type=jnp.float32))
                s = jnp.concatenate(parts, axis=1)
                peak = jnp.max(s, axis=-1, keepdims=True)
                prob = jnp.exp(s - peak).astype(jnp.bfloat16)
                o = jnp.dot(prob, va[...], preferred_element_type=jnp.float32)
                heads[sl, :] = jnp.where(mine, o[:, :C] / o[:, C:], heads[sl, :])
            return carry

        lax.fori_loop(0, HEADS, head, 0)
        rr = lax.broadcasted_iota(jnp.int32, (C, C), 0)
        cc = lax.broadcasted_iota(jnp.int32, (C, C), 1)
        part = jnp.dot(heads[...].astype(jnp.bfloat16), wout[...], preferred_element_type=jnp.float32)
        live = jnp.where(pad[:, pl.ds(off, PATCH)] > 0, 1.0, 0.0)
        for b in range(PATCH // C):
            diag = jnp.where(rr == cc, live[:, b * C : (b + 1) * C], 0.0).astype(jnp.bfloat16)
            col = jnp.dot(diag, jnp.ones((C, C), jnp.bfloat16), preferred_element_type=jnp.float32)
            at = pl.ds(off + b * C, C)
            out[at, :] = serial[at, :] + col * part[b * C : (b + 1) * C]
        return carry

    lax.fori_loop(0, rows // PATCH, patch, 0)


def attention(z_order, pad_mask, residual, gain, w_qkv, w_out):
    rows = residual.shape[0]
    vm = pl.BlockSpec(memory_space=pltpu.VMEM)
    return pl.pallas_call(
        attn_kernel,
        out_shape=jax.ShapeDtypeStruct((rows, C), jnp.float32),
        in_specs=[pl.BlockSpec(memory_space=pltpu.SMEM)] + [vm] * 5,
        out_specs=vm,
        scratch_shapes=[
            pltpu.VMEM((rows, C), jnp.float32),
            pltpu.VMEM((PATCH, C), jnp.bfloat16),
            pltpu.VMEM((2 * C, PATCH), jnp.bfloat16),
            pltpu.VMEM((PATCH, 2 * C), jnp.bfloat16),
            pltpu.VMEM((PATCH, C), jnp.float32),
            pltpu.VMEM((PATCH // QB, QB, QB), jnp.float32),
        ],
        compiler_params=pltpu.CompilerParams(vmem_limit_bytes=48 * 2**20),
        name="attention",
    )(z_order, pad_mask, residual, gain, w_qkv, w_out)


def moved_kernel(cap, per, hil, cnt, mixed, gain, wup, wdown, out, starts, rowbuf, send, send_sem, recv_sem, own_sem):
    n_x, n_y = lax.axis_size("gx"), lax.axis_size("gy")
    me_x, me_y = lax.axis_index("gx"), lax.axis_index("gy")
    me = me_x * n_y + me_y
    devices = n_x * n_y
    last = hil.shape[1] - 1

    def place(i):
        return lax.rem(me_x + i // n_y, n_x), lax.rem(me_y + i % n_y, n_y)

    barrier = pltpu.get_barrier_semaphore()

    def greet(i, carry):
        pl.semaphore_signal(barrier, inc=1, device_id=place(i), device_id_type=pl.DeviceIdType.MESH)
        return carry

    lax.fori_loop(1, devices, greet, 0)

    def offset(e, total):
        starts[e] = total
        return total + cnt[0, e]

    lax.fori_loop(0, devices, offset, jnp.int32(0))

    def compute(c):
        def rows_of(d, carry):
            to_x, to_y = place(c * per + d)
            start = starts[to_x * n_y + to_y]
            for j in range(cap):
                idx = hil[0, jnp.minimum(start + j, last)]
                rowbuf[pl.ds(d * cap + j, 1), :] = mixed[pl.ds(idx, 1), :]
            return carry

        lax.fori_loop(0, per, rows_of, 0)
        x = rowbuf[...]
        mlp_in = norm_rows(x, gain[...]).astype(jnp.bfloat16)
        up = jnp.dot(mlp_in, wup[...], preferred_element_type=jnp.float32)
        hidden = jax.nn.gelu(up).astype(jnp.bfloat16)
        y = x + jnp.dot(hidden, wdown[...], preferred_element_type=jnp.float32)
        slot = lax.broadcasted_iota(jnp.int32, (cap, C), 0)
        for d in range(per):
            to_x, to_y = place(c * per + d)
            count = cnt[0, to_x * n_y + to_y]
            send[c * per + d] = jnp.where(slot < count, y[d * cap : (d + 1) * cap], 0.0).astype(jnp.bfloat16)

    def copy(i):
        return pltpu.make_async_remote_copy(
            src_ref=send.at[i],
            dst_ref=out.at[me],
            send_sem=send_sem.at[i],
            recv_sem=recv_sem.at[i],
            device_id=place(i),
            device_id_type=pl.DeviceIdType.MESH,
        )

    def begin(i, carry):
        copy(i).start()
        return carry

    compute(0)
    own = pltpu.make_async_copy(send.at[0], out.at[me], own_sem)
    own.start()
    pl.semaphore_wait(barrier, devices - 1)
    lax.fori_loop(1, per, begin, 0)

    def step(c, carry):
        compute(c)
        lax.fori_loop(c * per, (c + 1) * per, begin, 0)
        return carry

    lax.fori_loop(1, devices // per, step, 0)
    own.wait()

    def finish(i, carry):
        copy(i).wait()
        return carry

    lax.fori_loop(1, devices, finish, 0)


def move_rows(hilbert_order, send_counts, mixed, gain, w_up, w_down, cap):
    devices = send_counts.shape[1]
    per = 8
    vm = pl.BlockSpec(memory_space=pltpu.VMEM)
    sm = pl.BlockSpec(memory_space=pltpu.SMEM)
    return pl.pallas_call(
        functools.partial(moved_kernel, cap, per),
        out_shape=jax.ShapeDtypeStruct((devices, cap, C), jnp.bfloat16),
        in_specs=[sm, sm] + [vm] * 4,
        out_specs=pl.BlockSpec(memory_space=pl.ANY),
        scratch_shapes=[
            pltpu.SMEM((devices,), jnp.int32),
            pltpu.VMEM((per * cap, C), jnp.float32),
            pltpu.VMEM((devices, cap, C), jnp.bfloat16),
            pltpu.SemaphoreType.DMA((devices,)),
            pltpu.SemaphoreType.DMA((devices,)),
            pltpu.SemaphoreType.DMA,
        ],
        compiler_params=pltpu.CompilerParams(
            vmem_limit_bytes=48 * 2**20, collective_id=1, has_side_effects=True
        ),
        name="move_rows",
    )(hilbert_order, send_counts, mixed, gain, w_up, w_down)


def padded(x, sides, width):
    for axis, dim in sides:
        devices, length = (lax.axis_size(axis), x.shape[dim])
        up = [(i, (i + 1) % devices) for i in range(devices - 1)]
        down = [(j, i) for i, j in up]
        last = lax.slice_in_dim(x, length - width, length, axis=dim)
        initial = lax.slice_in_dim(x, 0, width, axis=dim)
        before = lax.ppermute(last, axis, up)
        after = lax.ppermute(initial, axis, down)
        x = jnp.concatenate([before, x, after], axis=dim)
    return x


def body(
    points,
    occupied,
    z_order,
    pad_mask,
    hilbert_order,
    send_counts,
    w_conv,
    cpe_proj,
    cpe_gain,
    attn_gain,
    w_qkv,
    w_out,
    mlp_gain,
    w_up,
    w_down,
):
    point_count, width = points.shape
    depth = point_count // (LA * LB)
    filled = jnp.where(occupied[:, None] > 0, points, jnp.zeros_like(points))
    voxels = filled.reshape(LA, LB, depth, width)
    window = padded(voxels, (("gx", 0), ("gy", 1)), 1)
    window = jnp.pad(window, ((0, 0), (0, 0), (1, 1), (0, 0)))
    conv_sum = jnp.zeros((point_count, width), jnp.float32)
    for step_a in range(3):
        for step_b in range(3):
            for step_z in range(3):
                tap = step_a * 9 + step_b * 3 + step_z
                piece = window[
                    step_a : step_a + LA, step_b : step_b + LB, step_z : step_z + depth
                ].reshape(point_count, width)
                conv_sum = conv_sum + jnp.dot(
                    piece, w_conv[tap], preferred_element_type=jnp.float32
                )
    conv_out = conv_sum.astype(jnp.bfloat16)
    encoded = norm_rows(jnp.dot(conv_out, cpe_proj, preferred_element_type=jnp.float32), cpe_gain)
    residual = points.astype(jnp.float32) + encoded
    mixed = attention(
        z_order, pad_mask, residual, attn_gain.reshape(1, width), w_qkv, w_out
    )
    device_total = lax.axis_size("gx") * lax.axis_size("gy")
    capacity = point_count // device_total + max(2, point_count // (4 * device_total))
    received = move_rows(
        hilbert_order, send_counts, mixed, mlp_gain.reshape(1, width), w_up, w_down, capacity
    )
    return received.reshape(device_total * capacity, width)


def solution(mesh):
    placed = (
        P(("gx", "gy"), None),
        P(("gx", "gy")),
        P(("gx", "gy"), None),
        P(("gx", "gy"), None),
        P(("gx", "gy"), None),
        P(("gx", "gy"), None),
        P(),
        P(),
        P(),
        P(),
        P(),
        P(),
        P(),
        P(),
        P(),
    )
    return jax.shard_map(
        body, mesh=mesh, in_specs=placed, out_specs=P(("gx", "gy"), None), check_vma=False
    )
```

```python
import functools
import jax
import jax.numpy as jnp
from jax import lax
from jax.experimental import pallas as pl
from jax.experimental.pallas import tpu as pltpu
from jax.sharding import PartitionSpec as P

C = 128
LA = 16
LB = 16
HEADS = 8
PATCH = 1024
HEAD_DIM = 16
QB = 256


def norm_rows(v, gain):
    center = v - jnp.mean(v, axis=-1, keepdims=True)
    spread = jnp.mean(center * center, axis=-1, keepdims=True)
    return center * lax.rsqrt(spread + 1e-05) * gain


def attn_kernel(zord, pad, res, gain, wqkv, wout, out, serial, qs, kt, va, heads, bd):
    rows = serial.shape[0]

    def gather(i, carry):
        base = i * 16
        for u in range(16):
            idx = zord[0, base + u]
            serial[pl.ds(base + u, 1), :] = res[pl.ds(idx, 1), :]
        return carry

    lax.fori_loop(0, rows // 16, gather, 0)

    va[:, C:] = jnp.ones((PATCH, C), jnp.bfloat16)
    sub = lax.broadcasted_iota(jnp.int32, (C, PATCH), 0)

    def patch(p, carry):
        off = pl.multiple_of(p * PATCH, PATCH)
        attn_in = norm_rows(serial[pl.ds(off, PATCH), :], gain[...]).astype(jnp.bfloat16)
        proj = jnp.dot(attn_in, wqkv[...], preferred_element_type=jnp.float32).astype(jnp.bfloat16)
        qs[...] = proj[:, :C] * jnp.bfloat16(HEAD_DIM ** -0.5)
        kt[:C, :] = proj[:, C : 2 * C].T
        va[:, :C] = proj[:, 2 * C :]
        bias = jnp.where(pad[:, pl.ds(off, PATCH)] > 0, 0.0, -1e30)
        kt[C:, :] = jnp.where(sub == 0, jnp.broadcast_to(bias, (C, PATCH)), 0.0).astype(jnp.bfloat16)
        rr = lax.broadcasted_iota(jnp.int32, (QB, QB), 0)
        cc = lax.broadcasted_iota(jnp.int32, (QB, QB), 1)
        for b in range(PATCH // QB):
            bd[b] = jnp.where(rr == cc, 0.0, bias[:, b * QB : (b + 1) * QB])

        def head(h, carry):
            lane = lax.broadcasted_iota(jnp.int32, (QB, C), 1)
            mine = lane // HEAD_DIM == h
            one = jnp.where(lane == 0, 1.0, 0.0).astype(jnp.bfloat16)
            for b in range(PATCH // QB):
                sl = slice(b * QB, (b + 1) * QB)
                q = jnp.where(mine, qs[sl, :], jnp.bfloat16(0))
                qa = jnp.concatenate([q, one], axis=1)
                parts = []
                for t in range(PATCH // QB):
                    ts = slice(t * QB, (t + 1) * QB)
                    if t == b:
                        parts.append(
                            jnp.dot(q, kt[:C, ts], preferred_element_type=jnp.float32) + bd[b]
                        )
                    else:
                        parts.append(jnp.dot(qa, kt[:, ts], preferred_element_type=jnp.float32))
                s = jnp.concatenate(parts, axis=1)
                peak = jnp.max(s, axis=-1, keepdims=True)
                prob = jnp.exp(s - peak).astype(jnp.bfloat16)
                o = jnp.dot(prob, va[...], preferred_element_type=jnp.float32)
                heads[sl, :] = jnp.where(mine, o[:, :C] / o[:, C:], heads[sl, :])
            return carry

        lax.fori_loop(0, HEADS, head, 0)
        rr = lax.broadcasted_iota(jnp.int32, (C, C), 0)
        cc = lax.broadcasted_iota(jnp.int32, (C, C), 1)
        part = jnp.dot(heads[...].astype(jnp.bfloat16), wout[...], preferred_element_type=jnp.float32)
        live = jnp.where(pad[:, pl.ds(off, PATCH)] > 0, 1.0, 0.0)
        for b in range(PATCH // C):
            diag = jnp.where(rr == cc, live[:, b * C : (b + 1) * C], 0.0).astype(jnp.bfloat16)
            col = jnp.dot(diag, jnp.ones((C, C), jnp.bfloat16), preferred_element_type=jnp.float32)
            at = pl.ds(off + b * C, C)
            out[at, :] = serial[at, :] + col * part[b * C : (b + 1) * C]
        return carry

    lax.fori_loop(0, rows // PATCH, patch, 0)


def attention(z_order, pad_mask, residual, gain, w_qkv, w_out):
    rows = residual.shape[0]
    vm = pl.BlockSpec(memory_space=pltpu.VMEM)
    return pl.pallas_call(
        attn_kernel,
        out_shape=jax.ShapeDtypeStruct((rows, C), jnp.float32),
        in_specs=[pl.BlockSpec(memory_space=pltpu.SMEM)] + [vm] * 5,
        out_specs=vm,
        scratch_shapes=[
            pltpu.VMEM((rows, C), jnp.float32),
            pltpu.VMEM((PATCH, C), jnp.bfloat16),
            pltpu.VMEM((2 * C, PATCH), jnp.bfloat16),
            pltpu.VMEM((PATCH, 2 * C), jnp.bfloat16),
            pltpu.VMEM((PATCH, C), jnp.float32),
            pltpu.VMEM((PATCH // QB, QB, QB), jnp.float32),
        ],
        compiler_params=pltpu.CompilerParams(vmem_limit_bytes=48 * 2**20),
        name="attention",
    )(z_order, pad_mask, residual, gain, w_qkv, w_out)


def encode_kernel(pts, occ, wconv, proj, gain, out, win, taps, send_sem, recv_sem):
    n_x, n_y = lax.axis_size("gx"), lax.axis_size("gy")
    me_x, me_y = lax.axis_index("gx"), lax.axis_index("gy")
    z = pts.shape[2]
    cols = C // z
    sides = [(dx, dy) for dx in (-1, 0, 1) for dy in (-1, 0, 1) if (dx, dy) != (0, 0)]

    def place(dx, dy):
        return lax.rem(me_x + (dx + n_x), n_x), lax.rem(me_y + (dy + n_y), n_y)

    barrier = pltpu.get_barrier_semaphore()
    for dx, dy in sides:
        pl.semaphore_signal(barrier, inc=1, device_id=place(dx, dy), device_id_type=pl.DeviceIdType.MESH)

    rr = lax.broadcasted_iota(jnp.int32, (C, C), 0)
    cc = lax.broadcasted_iota(jnp.int32, (C, C), 1)

    def pick(dz, row):
        hit = (cc == rr + dz) & (rr // z == cc // z)
        return jnp.where(hit, row, 0.0).astype(jnp.bfloat16)

    def put(dz, a, b, block):
        win[dz + 1, a, b] = block.astype(jnp.bfloat16).reshape(block.shape[0] // z, z, C)

    def own_block(r):
        a, b = r // 2, lax.rem(r, 2) * cols
        row = jnp.where(occ[:, pl.ds(pl.multiple_of(r * C, C), C)] > 0, 1.0, 0.0)
        return a, b, row, pts[a, pl.ds(b, cols)].reshape(C, C)

    def fill(r, carry):
        a, b, row, block = own_block(r)
        put(0, a + 1, pl.ds(b + 1, cols), jnp.dot(pick(0, row), block, preferred_element_type=jnp.float32))
        return carry

    lax.fori_loop(0, LA * LB // cols, fill, 0)

    def span(d, n):
        here = {-1: pl.ds(1, 1), 0: pl.ds(1, n), 1: pl.ds(n, 1)}[d]
        there = {-1: pl.ds(n + 1, 1), 0: pl.ds(1, n), 1: pl.ds(0, 1)}[d]
        return here, there

    copies = []
    for k, (dx, dy) in enumerate(sides):
        (from_a, to_a), (from_b, to_b) = span(dx, LA), span(dy, LB)
        copies.append(
            pltpu.make_async_remote_copy(
                src_ref=win.at[1, from_a, from_b],
                dst_ref=win.at[1, to_a, to_b],
                send_sem=send_sem.at[k],
                recv_sem=recv_sem.at[k],
                device_id=place(dx, dy),
                device_id_type=pl.DeviceIdType.MESH,
            )
        )
    pl.semaphore_wait(barrier, len(sides))
    for copy in copies:
        copy.start()

    def shift(r, carry):
        a, b, row, block = own_block(r)
        for dz in (-1, 1):
            put(dz, a + 1, pl.ds(b + 1, cols), jnp.dot(pick(dz, row), block, preferred_element_type=jnp.float32))
        return carry

    lax.fori_loop(0, LA * LB // cols, shift, 0)

    none = jnp.zeros((C, C), jnp.bfloat16)
    for i in range(4):
        for sb in range(3):
            for sz in range(3):
                at = ((i * 3 + sb) * 3 + sz) * C
                taps[at : at + C, :C] = wconv[i * 9 + sb * 3 + sz] if i < 3 else none
                taps[at : at + C, C:] = wconv[(i - 1) * 9 + sb * 3 + sz] if i > 0 else none

    for copy in copies:
        copy.wait()

    low_x = jnp.where(me_x > 0, 1.0, 0.0)
    high_x = jnp.where(me_x < n_x - 1, 1.0, 0.0)
    low_y = jnp.where(me_y > 0, 1.0, 0.0)
    high_y = jnp.where(me_y < n_y - 1, 1.0, 0.0)

    def edge(a, b, count, live):
        block = win[1, a, b].reshape(count * z, C)
        for dz in (-1, 0, 1):
            mat = pick(dz, live)[: count * z, : count * z]
            put(dz, a, b, jnp.dot(mat, block, preferred_element_type=jnp.float32))

    for half in range(2):
        run = pl.ds(1 + half * cols, cols)
        edge(0, run, cols, low_x)
        edge(LA + 1, run, cols, high_x)
        edge(run, 0, cols, low_y)
        edge(run, LB + 1, cols, high_y)
    for a, live_x in ((0, low_x), (LA + 1, high_x)):
        for b, live_y in ((0, low_y), (LB + 1, high_y)):
            edge(a, pl.ds(b, 1), 1, live_x * live_y)

    tall = 2
    wide = LB * z

    def conv(t, carry):
        total = None
        for sb in range(3):
            for pair in range(2):
                pieces = []
                for i in (2 * pair, 2 * pair + 1):
                    for sz in range(3):
                        pieces.append(
                            jnp.concatenate(
                                [
                                    win[sz, (t * tall + u) * 2 + i, sb : sb + LB].reshape(wide, C)
                                    for u in range(tall)
                                ],
                                axis=0,
                            )
                        )
                w = jnp.concatenate(
                    [taps[((i * 3 + sb) * 3) * C : ((i * 3 + sb) * 3 + 3) * C, :] for i in (2 * pair, 2 * pair + 1)],
                    axis=0,
                )
                term = jnp.dot(jnp.concatenate(pieces, axis=1), w, preferred_element_type=jnp.float32)
                total = term if total is None else total + term
        for o in range(2):
            conv_out = total[:, o * C : (o + 1) * C].astype(jnp.bfloat16)
            encoded = norm_rows(
                jnp.dot(conv_out, proj[...], preferred_element_type=jnp.float32), gain[...]
            )
            for u in range(tall):
                a = (t * tall + u) * 2 + o
                out[pl.ds(pl.multiple_of(a * wide, wide), wide), :] = (
                    pts[a].reshape(wide, C).astype(jnp.float32) + encoded[u * wide : (u + 1) * wide]
                )
        return carry

    lax.fori_loop(0, LA // 2 // tall, conv, 0)


def encode(points, occupied, w_conv, cpe_proj, gain):
    rows = points.shape[0]
    depth = rows // (LA * LB)
    vm = pl.BlockSpec(memory_space=pltpu.VMEM)
    return pl.pallas_call(
        encode_kernel,
        out_shape=jax.ShapeDtypeStruct((rows, C), jnp.float32),
        in_specs=[vm] * 5,
        out_specs=vm,
        scratch_shapes=[
            pltpu.VMEM((3, LA + 2, LB + 2, depth, C), jnp.bfloat16),
            pltpu.VMEM((36 * C, 2 * C), jnp.bfloat16),
            pltpu.SemaphoreType.DMA((8,)),
            pltpu.SemaphoreType.DMA((8,)),
        ],
        compiler_params=pltpu.CompilerParams(
            vmem_limit_bytes=48 * 2**20, collective_id=0, has_side_effects=True
        ),
        name="encode",
    )(points.reshape(LA, LB, depth, C), occupied.reshape(1, rows), w_conv, cpe_proj, gain)


def moved_kernel(cap, per, hil, cnt, mixed, gain, wup, wdown, out, starts, rowbuf, send, send_sem, recv_sem, own_sem):
    n_x, n_y = lax.axis_size("gx"), lax.axis_size("gy")
    me_x, me_y = lax.axis_index("gx"), lax.axis_index("gy")
    me = me_x * n_y + me_y
    devices = n_x * n_y
    last = hil.shape[1] - 1

    def place(i):
        return lax.rem(me_x + i // n_y, n_x), lax.rem(me_y + i % n_y, n_y)

    barrier = pltpu.get_barrier_semaphore()

    def greet(i, carry):
        pl.semaphore_signal(barrier, inc=1, device_id=place(i), device_id_type=pl.DeviceIdType.MESH)
        return carry

    lax.fori_loop(1, devices, greet, 0)

    def offset(e, total):
        starts[e] = total
        return total + cnt[0, e]

    lax.fori_loop(0, devices, offset, jnp.int32(0))

    def compute(c):
        def rows_of(d, carry):
            to_x, to_y = place(c * per + d)
            start = starts[to_x * n_y + to_y]
            for j in range(cap):
                idx = hil[0, jnp.minimum(start + j, last)]
                rowbuf[pl.ds(d * cap + j, 1), :] = mixed[pl.ds(idx, 1), :]
            return carry

        lax.fori_loop(0, per, rows_of, 0)
        x = rowbuf[...]
        mlp_in = norm_rows(x, gain[...]).astype(jnp.bfloat16)
        up = jnp.dot(mlp_in, wup[...], preferred_element_type=jnp.float32)
        hidden = jax.nn.gelu(up).astype(jnp.bfloat16)
        y = x + jnp.dot(hidden, wdown[...], preferred_element_type=jnp.float32)
        slot = lax.broadcasted_iota(jnp.int32, (cap, C), 0)
        for d in range(per):
            to_x, to_y = place(c * per + d)
            count = cnt[0, to_x * n_y + to_y]
            send[c * per + d] = jnp.where(slot < count, y[d * cap : (d + 1) * cap], 0.0).astype(jnp.bfloat16)

    def copy(i):
        return pltpu.make_async_remote_copy(
            src_ref=send.at[i],
            dst_ref=out.at[me],
            send_sem=send_sem.at[i],
            recv_sem=recv_sem.at[i],
            device_id=place(i),
            device_id_type=pl.DeviceIdType.MESH,
        )

    def begin(i, carry):
        copy(i).start()
        return carry

    compute(0)
    own = pltpu.make_async_copy(send.at[0], out.at[me], own_sem)
    own.start()
    pl.semaphore_wait(barrier, devices - 1)
    lax.fori_loop(1, per, begin, 0)

    def step(c, carry):
        compute(c)
        lax.fori_loop(c * per, (c + 1) * per, begin, 0)
        return carry

    lax.fori_loop(1, devices // per, step, 0)
    own.wait()

    def finish(i, carry):
        copy(i).wait()
        return carry

    lax.fori_loop(1, devices, finish, 0)


def move_rows(hilbert_order, send_counts, mixed, gain, w_up, w_down, cap):
    devices = send_counts.shape[1]
    per = 8
    vm = pl.BlockSpec(memory_space=pltpu.VMEM)
    sm = pl.BlockSpec(memory_space=pltpu.SMEM)
    return pl.pallas_call(
        functools.partial(moved_kernel, cap, per),
        out_shape=jax.ShapeDtypeStruct((devices, cap, C), jnp.bfloat16),
        in_specs=[sm, sm] + [vm] * 4,
        out_specs=pl.BlockSpec(memory_space=pl.ANY),
        scratch_shapes=[
            pltpu.SMEM((devices,), jnp.int32),
            pltpu.VMEM((per * cap, C), jnp.float32),
            pltpu.VMEM((devices, cap, C), jnp.bfloat16),
            pltpu.SemaphoreType.DMA((devices,)),
            pltpu.SemaphoreType.DMA((devices,)),
            pltpu.SemaphoreType.DMA,
        ],
        compiler_params=pltpu.CompilerParams(
            vmem_limit_bytes=48 * 2**20, collective_id=1, has_side_effects=True
        ),
        name="move_rows",
    )(hilbert_order, send_counts, mixed, gain, w_up, w_down)


def body(
    points,
    occupied,
    z_order,
    pad_mask,
    hilbert_order,
    send_counts,
    w_conv,
    cpe_proj,
    cpe_gain,
    attn_gain,
    w_qkv,
    w_out,
    mlp_gain,
    w_up,
    w_down,
):
    point_count, width = points.shape
    residual = encode(points, occupied, w_conv, cpe_proj, cpe_gain.reshape(1, width))
    mixed = attention(
        z_order, pad_mask, residual, attn_gain.reshape(1, width), w_qkv, w_out
    )
    device_total = lax.axis_size("gx") * lax.axis_size("gy")
    capacity = point_count // device_total + max(2, point_count // (4 * device_total))
    received = move_rows(
        hilbert_order, send_counts, mixed, mlp_gain.reshape(1, width), w_up, w_down, capacity
    )
    return received.reshape(device_total * capacity, width)


def solution(mesh):
    placed = (
        P(("gx", "gy"), None),
        P(("gx", "gy")),
        P(("gx", "gy"), None),
        P(("gx", "gy"), None),
        P(("gx", "gy"), None),
        P(("gx", "gy"), None),
        P(),
        P(),
        P(),
        P(),
        P(),
        P(),
        P(),
        P(),
        P(),
    )
    return jax.shard_map(
        body, mesh=mesh, in_specs=placed, out_specs=P(("gx", "gy"), None), check_vma=False
    )
```

```python
import functools
import math
import jax
import jax.numpy as jnp
from jax import lax
from jax.experimental import pallas as pl
from jax.experimental.pallas import tpu as pltpu
from jax.sharding import PartitionSpec as P

C = 128
LA = 16
LB = 16
HEADS = 8
PATCH = 1024
HEAD_DIM = 16
QB = 256
UNROLL = 2


def norm_rows(v, gain):
    center = v - jnp.mean(v, axis=-1, keepdims=True)
    spread = jnp.mean(center * center, axis=-1, keepdims=True)
    return center * lax.rsqrt(spread + 1e-05) * gain


def attn_kernel(zord, pad, res, gain, wqkv, wout, out, serial, qw, ka, vt, heads, live, bd, sbuf):
    rows = serial.shape[0]
    blocks = PATCH // QB
    half = C // 2

    def gather(i, carry):
        base = i * 16
        for u in range(16):
            idx = zord[0, base + u]
            serial[pl.ds(base + u, 1), :] = res[pl.ds(idx, 1), :]
        return carry

    lax.fori_loop(0, rows // 16, gather, 0)

    first = lax.broadcasted_iota(jnp.int32, (HEAD_DIM, PATCH), 0) == 0
    unit = jnp.where(first, 1.0, 0.0).astype(jnp.bfloat16)
    for h in range(HEADS):
        qw[h] = jnp.zeros((2 * C, PATCH), jnp.bfloat16)
        qw[h, 3 * half : 3 * half + HEAD_DIM] = unit
        vt[h, HEAD_DIM:] = unit

    def patch(p, carry):
        off = pl.multiple_of(p * PATCH, PATCH)
        attn_in = norm_rows(serial[pl.ds(off, PATCH), :], gain[...]).astype(jnp.bfloat16)
        proj = jnp.dot(attn_in, wqkv[...], preferred_element_type=jnp.float32)
        proj = proj.astype(jnp.bfloat16).astype(jnp.float32)
        qt = proj[:, :C].T * jnp.float32(HEAD_DIM ** -0.5 * math.log2(math.e))
        high = qt.astype(jnp.bfloat16)
        rest = qt - high.astype(jnp.float32)
        mid = rest.astype(jnp.bfloat16)
        low = (rest - mid.astype(jnp.float32)).astype(jnp.bfloat16)
        vals = proj[:, 2 * C :].T.astype(jnp.bfloat16)
        for h in range(HEADS):
            sl = slice(h * HEAD_DIM, (h + 1) * HEAD_DIM)
            at = h % 4 * HEAD_DIM
            qw[h, at : at + HEAD_DIM] = high[sl]
            qw[h, half + at : half + at + HEAD_DIM] = mid[sl]
            qw[h, C + at : C + at + HEAD_DIM] = low[sl]
            vt[h, :HEAD_DIM] = vals[sl]
        rr = lax.broadcasted_iota(jnp.int32, (C, C), 0)
        cc = lax.broadcasted_iota(jnp.int32, (C, C), 1)
        real = jnp.where(pad[:, pl.ds(off, PATCH)] > 0, 1.0, 0.0)
        for b in range(PATCH // C):
            diag = jnp.where(rr == cc, real[:, b * C : (b + 1) * C], 0.0).astype(jnp.bfloat16)
            live[b * C : (b + 1) * C] = jnp.dot(
                diag, jnp.ones((C, C), jnp.bfloat16), preferred_element_type=jnp.float32
            )
        bias = (1.0 - live[...]) * -1e30
        k = proj[:, C : 2 * C]
        kr = pltpu.roll(k, half, 1)
        left = lax.broadcasted_iota(jnp.int32, (PATCH, C), 1) < half
        ka[0, :, :C] = jnp.where(left, k, kr).astype(jnp.bfloat16)
        ka[0, :, C:] = jnp.where(left, k, bias).astype(jnp.bfloat16)
        ka[1, :, :C] = jnp.where(left, kr, k).astype(jnp.bfloat16)
        ka[1, :, C:] = jnp.where(left, kr, bias).astype(jnp.bfloat16)
        rr = lax.broadcasted_iota(jnp.int32, (QB, QB), 0)
        cc = lax.broadcasted_iota(jnp.int32, (QB, QB), 1)
        for b in range(blocks):
            col = bias[b * QB : (b + 1) * QB]
            bd[b] = jnp.where(rr == cc, 0.0, jnp.concatenate([col, col], axis=1))

        def scores(h, b, t):
            g = h // 4
            qs = slice(b * QB, (b + 1) * QB)
            ts = slice(t * QB, (t + 1) * QB)
            if t == b:
                w = jnp.concatenate(
                    [qw[h, : 3 * half, qs], jnp.zeros((half, QB), jnp.bfloat16)], axis=0
                )
                s = jnp.dot(ka[g, ts], w, preferred_element_type=jnp.float32) + bd[b]
            else:
                s = jnp.dot(ka[g, ts], qw[h, :, qs], preferred_element_type=jnp.float32)
            sbuf[b % 2, ts] = s
            return jnp.max(s.reshape(QB // 8, 8, QB), axis=0)

        def values(h, b, t, peak):
            ts = slice(t * QB, (t + 1) * QB)
            prob = jnp.exp2(sbuf[b % 2, ts] - peak).astype(jnp.bfloat16)
            return jnp.dot(vt[h, :, ts], prob, preferred_element_type=jnp.float32)

        def top(parts):
            m = functools.reduce(jnp.maximum, parts)
            return jnp.max(m, axis=0, keepdims=True)

        start = top([scores(0, 0, t) for t in range(blocks)])

        def head(h, peak):
            for b in range(blocks):
                h2, b2 = (h, b + 1) if b + 1 < blocks else (lax.rem(h + 1, HEADS), 0)
                parts = []
                total = None
                for t in range(blocks):
                    parts.append(scores(h2, b2, t))
                    term = values(h, b, t, peak)
                    total = term if total is None else total + term
                heads[pl.ds(pl.multiple_of(h * HEAD_DIM, HEAD_DIM), HEAD_DIM), b * QB : (b + 1) * QB] = (
                    total[:HEAD_DIM] / total[HEAD_DIM : HEAD_DIM + 1]
                )
                peak = top(parts)
            return peak

        lax.fori_loop(0, HEADS, head, start, unroll=UNROLL)
        mixed_heads = heads[...].T.astype(jnp.bfloat16)
        part = jnp.dot(mixed_heads, wout[...], preferred_element_type=jnp.float32)
        at = pl.ds(off, PATCH)
        out[at, :] = serial[at, :] + live[...] * part
        return carry

    lax.fori_loop(0, rows // PATCH, patch, 0)


def attention(z_order, pad_mask, residual, gain, w_qkv, w_out):
    rows = residual.shape[0]
    vm = pl.BlockSpec(memory_space=pltpu.VMEM)
    return pl.pallas_call(
        attn_kernel,
        out_shape=jax.ShapeDtypeStruct((rows, C), jnp.float32),
        in_specs=[pl.BlockSpec(memory_space=pltpu.SMEM)] + [vm] * 5,
        out_specs=vm,
        scratch_shapes=[
            pltpu.VMEM((rows, C), jnp.float32),
            pltpu.VMEM((HEADS, 2 * C, PATCH), jnp.bfloat16),
            pltpu.VMEM((2, PATCH, 2 * C), jnp.bfloat16),
            pltpu.VMEM((HEADS, 2 * HEAD_DIM, PATCH), jnp.bfloat16),
            pltpu.VMEM((C, PATCH), jnp.float32),
            pltpu.VMEM((PATCH, C), jnp.float32),
            pltpu.VMEM((PATCH // QB, QB, QB), jnp.float32),
            pltpu.VMEM((2, PATCH, QB), jnp.float32),
        ],
        compiler_params=pltpu.CompilerParams(vmem_limit_bytes=48 * 2**20),
        name="attention",
    )(z_order, pad_mask, residual, gain, w_qkv, w_out)


def encode_kernel(pts, occ, wconv, proj, gain, out, win, taps, send_sem, recv_sem):
    n_x, n_y = lax.axis_size("gx"), lax.axis_size("gy")
    me_x, me_y = lax.axis_index("gx"), lax.axis_index("gy")
    z = pts.shape[2]
    cols = C // z
    sides = [(dx, dy) for dx in (-1, 0, 1) for dy in (-1, 0, 1) if (dx, dy) != (0, 0)]

    def place(dx, dy):
        return lax.rem(me_x + (dx + n_x), n_x), lax.rem(me_y + (dy + n_y), n_y)

    barrier = pltpu.get_barrier_semaphore()
    for dx, dy in sides:
        pl.semaphore_signal(barrier, inc=1, device_id=place(dx, dy), device_id_type=pl.DeviceIdType.MESH)

    rr = lax.broadcasted_iota(jnp.int32, (C, C), 0)
    cc = lax.broadcasted_iota(jnp.int32, (C, C), 1)

    def pick(dz, row):
        hit = (cc == rr + dz) & (rr // z == cc // z)
        return jnp.where(hit, row, 0.0).astype(jnp.bfloat16)

    def put(dz, a, b, block):
        win[dz + 1, a, b] = block.astype(jnp.bfloat16).reshape(block.shape[0] // z, z, C)

    def own_block(r):
        a, b = r // 2, lax.rem(r, 2) * cols
        row = jnp.where(occ[:, pl.ds(pl.multiple_of(r * C, C), C)] > 0, 1.0, 0.0)
        return a, b, row, pts[a, pl.ds(b, cols)].reshape(C, C)

    def fill(r, carry):
        a, b, row, block = own_block(r)
        put(0, a + 1, pl.ds(b + 1, cols), jnp.dot(pick(0, row), block, preferred_element_type=jnp.float32))
        return carry

    lax.fori_loop(0, LA * LB // cols, fill, 0)

    def span(d, n):
        here = {-1: pl.ds(1, 1), 0: pl.ds(1, n), 1: pl.ds(n, 1)}[d]
        there = {-1: pl.ds(n + 1, 1), 0: pl.ds(1, n), 1: pl.ds(0, 1)}[d]
        return here, there

    copies = []
    for k, (dx, dy) in enumerate(sides):
        (from_a, to_a), (from_b, to_b) = span(dx, LA), span(dy, LB)
        copies.append(
            pltpu.make_async_remote_copy(
                src_ref=win.at[1, from_a, from_b],
                dst_ref=win.at[1, to_a, to_b],
                send_sem=send_sem.at[k],
                recv_sem=recv_sem.at[k],
                device_id=place(dx, dy),
                device_id_type=pl.DeviceIdType.MESH,
            )
        )
    pl.semaphore_wait(barrier, len(sides))
    for copy in copies:
        copy.start()

    def shift(r, carry):
        a, b, row, block = own_block(r)
        for dz in (-1, 1):
            put(dz, a + 1, pl.ds(b + 1, cols), jnp.dot(pick(dz, row), block, preferred_element_type=jnp.float32))
        return carry

    lax.fori_loop(0, LA * LB // cols, shift, 0)

    none = jnp.zeros((C, C), jnp.bfloat16)
    for i in range(4):
        for sb in range(3):
            for sz in range(3):
                at = ((i * 3 + sb) * 3 + sz) * C
                taps[at : at + C, :C] = wconv[i * 9 + sb * 3 + sz] if i < 3 else none
                taps[at : at + C, C:] = wconv[(i - 1) * 9 + sb * 3 + sz] if i > 0 else none

    for copy in copies:
        copy.wait()

    low_x = jnp.where(me_x > 0, 1.0, 0.0)
    high_x = jnp.where(me_x < n_x - 1, 1.0, 0.0)
    low_y = jnp.where(me_y > 0, 1.0, 0.0)
    high_y = jnp.where(me_y < n_y - 1, 1.0, 0.0)

    def edge(a, b, count, live):
        block = win[1, a, b].reshape(count * z, C)
        for dz in (-1, 0, 1):
            mat = pick(dz, live)[: count * z, : count * z]
            put(dz, a, b, jnp.dot(mat, block, preferred_element_type=jnp.float32))

    for half in range(2):
        run = pl.ds(1 + half * cols, cols)
        edge(0, run, cols, low_x)
        edge(LA + 1, run, cols, high_x)
        edge(run, 0, cols, low_y)
        edge(run, LB + 1, cols, high_y)
    for a, live_x in ((0, low_x), (LA + 1, high_x)):
        for b, live_y in ((0, low_y), (LB + 1, high_y)):
            edge(a, pl.ds(b, 1), 1, live_x * live_y)

    tall = 2
    wide = LB * z

    def conv(t, carry):
        total = None
        for sb in range(3):
            for pair in range(2):
                pieces = []
                for i in (2 * pair, 2 * pair + 1):
                    for sz in range(3):
                        pieces.append(
                            jnp.concatenate(
                                [
                                    win[sz, (t * tall + u) * 2 + i, sb : sb + LB].reshape(wide, C)
                                    for u in range(tall)
                                ],
                                axis=0,
                            )
                        )
                w = jnp.concatenate(
                    [taps[((i * 3 + sb) * 3) * C : ((i * 3 + sb) * 3 + 3) * C, :] for i in (2 * pair, 2 * pair + 1)],
                    axis=0,
                )
                term = jnp.dot(jnp.concatenate(pieces, axis=1), w, preferred_element_type=jnp.float32)
                total = term if total is None else total + term
        for o in range(2):
            conv_out = total[:, o * C : (o + 1) * C].astype(jnp.bfloat16)
            encoded = norm_rows(
                jnp.dot(conv_out, proj[...], preferred_element_type=jnp.float32), gain[...]
            )
            for u in range(tall):
                a = (t * tall + u) * 2 + o
                out[pl.ds(pl.multiple_of(a * wide, wide), wide), :] = (
                    pts[a].reshape(wide, C).astype(jnp.float32) + encoded[u * wide : (u + 1) * wide]
                )
        return carry

    lax.fori_loop(0, LA // 2 // tall, conv, 0)


def encode(points, occupied, w_conv, cpe_proj, gain):
    rows = points.shape[0]
    depth = rows // (LA * LB)
    vm = pl.BlockSpec(memory_space=pltpu.VMEM)
    return pl.pallas_call(
        encode_kernel,
        out_shape=jax.ShapeDtypeStruct((rows, C), jnp.float32),
        in_specs=[vm] * 5,
        out_specs=vm,
        scratch_shapes=[
            pltpu.VMEM((3, LA + 2, LB + 2, depth, C), jnp.bfloat16),
            pltpu.VMEM((36 * C, 2 * C), jnp.bfloat16),
            pltpu.SemaphoreType.DMA((8,)),
            pltpu.SemaphoreType.DMA((8,)),
        ],
        compiler_params=pltpu.CompilerParams(
            vmem_limit_bytes=48 * 2**20, collective_id=0, has_side_effects=True
        ),
        name="encode",
    )(points.reshape(LA, LB, depth, C), occupied.reshape(1, rows), w_conv, cpe_proj, gain)


def moved_kernel(cap, per, hil, cnt, mixed, gain, wup, wdown, out, starts, rowbuf, send, send_sem, recv_sem, own_sem):
    n_x, n_y = lax.axis_size("gx"), lax.axis_size("gy")
    me_x, me_y = lax.axis_index("gx"), lax.axis_index("gy")
    me = me_x * n_y + me_y
    devices = n_x * n_y
    last = hil.shape[1] - 1

    def place(i):
        return lax.rem(me_x + i // n_y, n_x), lax.rem(me_y + i % n_y, n_y)

    barrier = pltpu.get_barrier_semaphore()

    def greet(i, carry):
        pl.semaphore_signal(barrier, inc=1, device_id=place(i), device_id_type=pl.DeviceIdType.MESH)
        return carry

    lax.fori_loop(1, devices, greet, 0)

    def offset(e, total):
        starts[e] = total
        return total + cnt[0, e]

    lax.fori_loop(0, devices, offset, jnp.int32(0))

    def compute(c):
        def rows_of(d, carry):
            to_x, to_y = place(c * per + d)
            start = starts[to_x * n_y + to_y]
            for j in range(cap):
                idx = hil[0, jnp.minimum(start + j, last)]
                rowbuf[pl.ds(d * cap + j, 1), :] = mixed[pl.ds(idx, 1), :]
            return carry

        lax.fori_loop(0, per, rows_of, 0)
        x = rowbuf[...]
        mlp_in = norm_rows(x, gain[...]).astype(jnp.bfloat16)
        up = jnp.dot(mlp_in, wup[...], preferred_element_type=jnp.float32)
        hidden = jax.nn.gelu(up).astype(jnp.bfloat16)
        y = x + jnp.dot(hidden, wdown[...], preferred_element_type=jnp.float32)
        slot = lax.broadcasted_iota(jnp.int32, (cap, C), 0)
        for d in range(per):
            to_x, to_y = place(c * per + d)
            count = cnt[0, to_x * n_y + to_y]
            send[c * per + d] = jnp.where(slot < count, y[d * cap : (d + 1) * cap], 0.0).astype(jnp.bfloat16)

    def copy(i):
        return pltpu.make_async_remote_copy(
            src_ref=send.at[i],
            dst_ref=out.at[me],
            send_sem=send_sem.at[i],
            recv_sem=recv_sem.at[i],
            device_id=place(i),
            device_id_type=pl.DeviceIdType.MESH,
        )

    def begin(i, carry):
        copy(i).start()
        return carry

    compute(0)
    own = pltpu.make_async_copy(send.at[0], out.at[me], own_sem)
    own.start()
    pl.semaphore_wait(barrier, devices - 1)
    lax.fori_loop(1, per, begin, 0)

    def step(c, carry):
        compute(c)
        lax.fori_loop(c * per, (c + 1) * per, begin, 0)
        return carry

    lax.fori_loop(1, devices // per, step, 0)
    own.wait()

    def finish(i, carry):
        copy(i).wait()
        return carry

    lax.fori_loop(1, devices, finish, 0)


def move_rows(hilbert_order, send_counts, mixed, gain, w_up, w_down, cap):
    devices = send_counts.shape[1]
    per = 8
    vm = pl.BlockSpec(memory_space=pltpu.VMEM)
    sm = pl.BlockSpec(memory_space=pltpu.SMEM)
    return pl.pallas_call(
        functools.partial(moved_kernel, cap, per),
        out_shape=jax.ShapeDtypeStruct((devices, cap, C), jnp.bfloat16),
        in_specs=[sm, sm] + [vm] * 4,
        out_specs=pl.BlockSpec(memory_space=pl.ANY),
        scratch_shapes=[
            pltpu.SMEM((devices,), jnp.int32),
            pltpu.VMEM((per * cap, C), jnp.float32),
            pltpu.VMEM((devices, cap, C), jnp.bfloat16),
            pltpu.SemaphoreType.DMA((devices,)),
            pltpu.SemaphoreType.DMA((devices,)),
            pltpu.SemaphoreType.DMA,
        ],
        compiler_params=pltpu.CompilerParams(
            vmem_limit_bytes=48 * 2**20, collective_id=1, has_side_effects=True
        ),
        name="move_rows",
    )(hilbert_order, send_counts, mixed, gain, w_up, w_down)


def body(
    points,
    occupied,
    z_order,
    pad_mask,
    hilbert_order,
    send_counts,
    w_conv,
    cpe_proj,
    cpe_gain,
    attn_gain,
    w_qkv,
    w_out,
    mlp_gain,
    w_up,
    w_down,
):
    point_count, width = points.shape
    residual = encode(points, occupied, w_conv, cpe_proj, cpe_gain.reshape(1, width))
    mixed = attention(
        z_order, pad_mask, residual, attn_gain.reshape(1, width), w_qkv, w_out
    )
    device_total = lax.axis_size("gx") * lax.axis_size("gy")
    capacity = point_count // device_total + max(2, point_count // (4 * device_total))
    received = move_rows(
        hilbert_order, send_counts, mixed, mlp_gain.reshape(1, width), w_up, w_down, capacity
    )
    return received.reshape(device_total * capacity, width)


def solution(mesh):
    placed = (
        P(("gx", "gy"), None),
        P(("gx", "gy")),
        P(("gx", "gy"), None),
        P(("gx", "gy"), None),
        P(("gx", "gy"), None),
        P(("gx", "gy"), None),
        P(),
        P(),
        P(),
        P(),
        P(),
        P(),
        P(),
        P(),
        P(),
    )
    return jax.shard_map(
        body, mesh=mesh, in_specs=placed, out_specs=P(("gx", "gy"), None), check_vma=False
    )
```

```python
import functools
import math
import jax
import jax.numpy as jnp
from jax import lax
from jax.experimental import pallas as pl
from jax.experimental.pallas import tpu as pltpu
from jax.sharding import PartitionSpec as P

C = 128
LA = 16
LB = 16
HEADS = 8
PATCH = 1024
HEAD_DIM = 16
QB = 256
UNROLL = 2


def norm_rows(v, gain):
    center = v - jnp.mean(v, axis=-1, keepdims=True)
    spread = jnp.mean(center * center, axis=-1, keepdims=True)
    return center * lax.rsqrt(spread + 1e-05) * gain


def attn_kernel(zord, pad, res, gain, wqkv, wout, out, serial, qw, ka, vt, heads, live, bd, sbuf):
    rows = serial.shape[0]
    blocks = PATCH // QB
    half = C // 2

    def gather(i, carry):
        base = i * 16
        for u in range(16):
            idx = zord[0, base + u]
            serial[pl.ds(base + u, 1), :] = res[pl.ds(idx, 1), :]
        return carry

    lax.fori_loop(0, rows // 16, gather, 0)

    first = lax.broadcasted_iota(jnp.int32, (HEAD_DIM, PATCH), 0) == 0
    unit = jnp.where(first, 1.0, 0.0).astype(jnp.bfloat16)
    for h in range(HEADS):
        qw[h] = jnp.zeros((2 * C, PATCH), jnp.bfloat16)
        qw[h, 3 * half : 3 * half + HEAD_DIM] = unit
        vt[h, HEAD_DIM:] = unit

    def patch(p, carry):
        off = pl.multiple_of(p * PATCH, PATCH)
        attn_in = norm_rows(serial[pl.ds(off, PATCH), :], gain[...]).astype(jnp.bfloat16)
        proj = jnp.dot(attn_in, wqkv[...], preferred_element_type=jnp.float32)
        proj = proj.astype(jnp.bfloat16).astype(jnp.float32)
        qt = proj[:, :C].T * jnp.float32(HEAD_DIM ** -0.5 * math.log2(math.e))
        high = qt.astype(jnp.bfloat16)
        rest = qt - high.astype(jnp.float32)
        mid = rest.astype(jnp.bfloat16)
        low = (rest - mid.astype(jnp.float32)).astype(jnp.bfloat16)
        vals = proj[:, 2 * C :].T.astype(jnp.bfloat16)
        for h in range(HEADS):
            sl = slice(h * HEAD_DIM, (h + 1) * HEAD_DIM)
            at = h % 4 * HEAD_DIM
            qw[h, at : at + HEAD_DIM] = high[sl]
            qw[h, half + at : half + at + HEAD_DIM] = mid[sl]
            qw[h, C + at : C + at + HEAD_DIM] = low[sl]
            vt[h, :HEAD_DIM] = vals[sl]
        rr = lax.broadcasted_iota(jnp.int32, (C, C), 0)
        cc = lax.broadcasted_iota(jnp.int32, (C, C), 1)
        real = jnp.where(pad[:, pl.ds(off, PATCH)] > 0, 1.0, 0.0)
        for b in range(PATCH // C):
            diag = jnp.where(rr == cc, real[:, b * C : (b + 1) * C], 0.0).astype(jnp.bfloat16)
            live[b * C : (b + 1) * C] = jnp.dot(
                diag, jnp.ones((C, C), jnp.bfloat16), preferred_element_type=jnp.float32
            )
        bias = (1.0 - live[...]) * -1e30
        k = proj[:, C : 2 * C]
        kr = pltpu.roll(k, half, 1)
        left = lax.broadcasted_iota(jnp.int32, (PATCH, C), 1) < half
        ka[0, :, :C] = jnp.where(left, k, kr).astype(jnp.bfloat16)
        ka[0, :, C:] = jnp.where(left, k, bias).astype(jnp.bfloat16)
        ka[1, :, :C] = jnp.where(left, kr, k).astype(jnp.bfloat16)
        ka[1, :, C:] = jnp.where(left, kr, bias).astype(jnp.bfloat16)
        rr = lax.broadcasted_iota(jnp.int32, (QB, QB), 0)
        cc = lax.broadcasted_iota(jnp.int32, (QB, QB), 1)
        for b in range(blocks):
            col = bias[b * QB : (b + 1) * QB]
            bd[b] = jnp.where(rr == cc, 0.0, jnp.concatenate([col, col], axis=1))

        def scores(h, b, t):
            g = h // 4
            qs = slice(b * QB, (b + 1) * QB)
            ts = slice(t * QB, (t + 1) * QB)
            if t == b:
                w = jnp.concatenate(
                    [qw[h, : 3 * half, qs], jnp.zeros((half, QB), jnp.bfloat16)], axis=0
                )
                s = jnp.dot(ka[g, ts], w, preferred_element_type=jnp.float32) + bd[b]
            else:
                s = jnp.dot(ka[g, ts], qw[h, :, qs], preferred_element_type=jnp.float32)
            sbuf[b % 2, ts] = s
            return jnp.max(s.reshape(QB // 8, 8, QB), axis=0)

        def values(h, b, t, peak):
            ts = slice(t * QB, (t + 1) * QB)
            prob = jnp.exp2(sbuf[b % 2, ts] - peak).astype(jnp.bfloat16)
            return jnp.dot(vt[h, :, ts], prob, preferred_element_type=jnp.float32)

        def top(parts):
            m = functools.reduce(jnp.maximum, parts)
            return jnp.max(m, axis=0, keepdims=True)

        start = top([scores(0, 0, t) for t in range(blocks)])

        def head(h, peak):
            for b in range(blocks):
                h2, b2 = (h, b + 1) if b + 1 < blocks else (lax.rem(h + 1, HEADS), 0)
                parts = []
                total = None
                for t in range(blocks):
                    parts.append(scores(h2, b2, t))
                    term = values(h, b, t, peak)
                    total = term if total is None else total + term
                heads[pl.ds(pl.multiple_of(h * HEAD_DIM, HEAD_DIM), HEAD_DIM), b * QB : (b + 1) * QB] = (
                    total[:HEAD_DIM] / total[HEAD_DIM : HEAD_DIM + 1]
                )
                peak = top(parts)
            return peak

        lax.fori_loop(0, HEADS, head, start, unroll=UNROLL)
        mixed_heads = heads[...].T.astype(jnp.bfloat16)
        part = jnp.dot(mixed_heads, wout[...], preferred_element_type=jnp.float32)
        at = pl.ds(off, PATCH)
        out[at, :] = serial[at, :] + live[...] * part
        return carry

    lax.fori_loop(0, rows // PATCH, patch, 0)


def attention(z_order, pad_mask, residual, gain, w_qkv, w_out):
    rows = residual.shape[0]
    vm = pl.BlockSpec(memory_space=pltpu.VMEM)
    return pl.pallas_call(
        attn_kernel,
        out_shape=jax.ShapeDtypeStruct((rows, C), jnp.float32),
        in_specs=[pl.BlockSpec(memory_space=pltpu.SMEM)] + [vm] * 5,
        out_specs=vm,
        scratch_shapes=[
            pltpu.VMEM((rows, C), jnp.float32),
            pltpu.VMEM((HEADS, 2 * C, PATCH), jnp.bfloat16),
            pltpu.VMEM((2, PATCH, 2 * C), jnp.bfloat16),
            pltpu.VMEM((HEADS, 2 * HEAD_DIM, PATCH), jnp.bfloat16),
            pltpu.VMEM((C, PATCH), jnp.float32),
            pltpu.VMEM((PATCH, C), jnp.float32),
            pltpu.VMEM((PATCH // QB, QB, QB), jnp.float32),
            pltpu.VMEM((2, PATCH, QB), jnp.float32),
        ],
        compiler_params=pltpu.CompilerParams(vmem_limit_bytes=48 * 2**20),
        name="attention",
    )(z_order, pad_mask, residual, gain, w_qkv, w_out)


def encode_kernel(pts, occ, wconv, proj, gain, out, win, taps, send_sem, recv_sem):
    n_x, n_y = lax.axis_size("gx"), lax.axis_size("gy")
    me_x, me_y = lax.axis_index("gx"), lax.axis_index("gy")
    z = pts.shape[2]
    cols = C // z
    sides = [(dx, dy) for dx in (-1, 0, 1) for dy in (-1, 0, 1) if (dx, dy) != (0, 0)]

    def place(dx, dy):
        return lax.rem(me_x + (dx + n_x), n_x), lax.rem(me_y + (dy + n_y), n_y)

    barrier = pltpu.get_barrier_semaphore()
    for dx, dy in sides:
        pl.semaphore_signal(barrier, inc=1, device_id=place(dx, dy), device_id_type=pl.DeviceIdType.MESH)

    rr = lax.broadcasted_iota(jnp.int32, (C, C), 0)
    cc = lax.broadcasted_iota(jnp.int32, (C, C), 1)

    def pick(dz, row):
        hit = (cc == rr + dz) & (rr // z == cc // z)
        return jnp.where(hit, row, 0.0).astype(jnp.bfloat16)

    def put(dz, a, b, block):
        win[dz + 1, a, b] = block.astype(jnp.bfloat16).reshape(block.shape[0] // z, z, C)

    def own_block(r):
        a, b = r // 2, lax.rem(r, 2) * cols
        row = jnp.where(occ[:, pl.ds(pl.multiple_of(r * C, C), C)] > 0, 1.0, 0.0)
        return a, b, row, pts[a, pl.ds(b, cols)].reshape(C, C)

    def fill(r, carry):
        a, b, row, block = own_block(r)
        put(0, a + 1, pl.ds(b + 1, cols), jnp.dot(pick(0, row), block, preferred_element_type=jnp.float32))
        return carry

    lax.fori_loop(0, LA * LB // cols, fill, 0)

    def span(d, n):
        here = {-1: pl.ds(1, 1), 0: pl.ds(1, n), 1: pl.ds(n, 1)}[d]
        there = {-1: pl.ds(n + 1, 1), 0: pl.ds(1, n), 1: pl.ds(0, 1)}[d]
        return here, there

    copies = []
    for k, (dx, dy) in enumerate(sides):
        (from_a, to_a), (from_b, to_b) = span(dx, LA), span(dy, LB)
        copies.append(
            pltpu.make_async_remote_copy(
                src_ref=win.at[1, from_a, from_b],
                dst_ref=win.at[1, to_a, to_b],
                send_sem=send_sem.at[k],
                recv_sem=recv_sem.at[k],
                device_id=place(dx, dy),
                device_id_type=pl.DeviceIdType.MESH,
            )
        )
    pl.semaphore_wait(barrier, len(sides))
    for copy in copies:
        copy.start()

    def shift(r, carry):
        a, b, row, block = own_block(r)
        for dz in (-1, 1):
            put(dz, a + 1, pl.ds(b + 1, cols), jnp.dot(pick(dz, row), block, preferred_element_type=jnp.float32))
        return carry

    lax.fori_loop(0, LA * LB // cols, shift, 0)

    none = jnp.zeros((C, C), jnp.bfloat16)
    for i in range(4):
        for sb in range(3):
            for sz in range(3):
                at = ((i * 3 + sb) * 3 + sz) * C
                taps[at : at + C, :C] = wconv[i * 9 + sb * 3 + sz] if i < 3 else none
                taps[at : at + C, C:] = wconv[(i - 1) * 9 + sb * 3 + sz] if i > 0 else none

    for copy in copies:
        copy.wait()

    low_x = jnp.where(me_x > 0, 1.0, 0.0)
    high_x = jnp.where(me_x < n_x - 1, 1.0, 0.0)
    low_y = jnp.where(me_y > 0, 1.0, 0.0)
    high_y = jnp.where(me_y < n_y - 1, 1.0, 0.0)

    def edge(a, b, count, live):
        block = win[1, a, b].reshape(count * z, C)
        for dz in (-1, 0, 1):
            mat = pick(dz, live)[: count * z, : count * z]
            put(dz, a, b, jnp.dot(mat, block, preferred_element_type=jnp.float32))

    for half in range(2):
        run = pl.ds(1 + half * cols, cols)
        edge(0, run, cols, low_x)
        edge(LA + 1, run, cols, high_x)
        edge(run, 0, cols, low_y)
        edge(run, LB + 1, cols, high_y)
    for a, live_x in ((0, low_x), (LA + 1, high_x)):
        for b, live_y in ((0, low_y), (LB + 1, high_y)):
            edge(a, pl.ds(b, 1), 1, live_x * live_y)

    tall = 2
    wide = LB * z

    def conv(t, carry):
        total = None
        for sb in range(3):
            for pair in range(2):
                pieces = []
                for i in (2 * pair, 2 * pair + 1):
                    for sz in range(3):
                        pieces.append(
                            jnp.concatenate(
                                [
                                    win[sz, (t * tall + u) * 2 + i, sb : sb + LB].reshape(wide, C)
                                    for u in range(tall)
                                ],
                                axis=0,
                            )
                        )
                w = jnp.concatenate(
                    [taps[((i * 3 + sb) * 3) * C : ((i * 3 + sb) * 3 + 3) * C, :] for i in (2 * pair, 2 * pair + 1)],
                    axis=0,
                )
                term = jnp.dot(jnp.concatenate(pieces, axis=1), w, preferred_element_type=jnp.float32)
                total = term if total is None else total + term
        for o in range(2):
            conv_out = total[:, o * C : (o + 1) * C].astype(jnp.bfloat16)
            encoded = norm_rows(
                jnp.dot(conv_out, proj[...], preferred_element_type=jnp.float32), gain[...]
            )
            for u in range(tall):
                a = (t * tall + u) * 2 + o
                out[pl.ds(pl.multiple_of(a * wide, wide), wide), :] = (
                    pts[a].reshape(wide, C).astype(jnp.float32) + encoded[u * wide : (u + 1) * wide]
                )
        return carry

    lax.fori_loop(0, LA // 2 // tall, conv, 0)


def encode(points, occupied, w_conv, cpe_proj, gain):
    rows = points.shape[0]
    depth = rows // (LA * LB)
    vm = pl.BlockSpec(memory_space=pltpu.VMEM)
    return pl.pallas_call(
        encode_kernel,
        out_shape=jax.ShapeDtypeStruct((rows, C), jnp.float32),
        in_specs=[vm] * 5,
        out_specs=vm,
        scratch_shapes=[
            pltpu.VMEM((3, LA + 2, LB + 2, depth, C), jnp.bfloat16),
            pltpu.VMEM((36 * C, 2 * C), jnp.bfloat16),
            pltpu.SemaphoreType.DMA((8,)),
            pltpu.SemaphoreType.DMA((8,)),
        ],
        compiler_params=pltpu.CompilerParams(
            vmem_limit_bytes=48 * 2**20, collective_id=0, has_side_effects=True
        ),
        name="encode",
    )(points.reshape(LA, LB, depth, C), occupied.reshape(1, rows), w_conv, cpe_proj, gain)


def moved_kernel(cap, per, hil, cnt, mixed, gain, wup, wdown, out, order, starts, rowbuf, send, send_sem, recv_sem, own_sem, order_sem, side_sem):
    n_x, n_y = lax.axis_size("gx"), lax.axis_size("gy")
    me_x, me_y = lax.axis_index("gx"), lax.axis_index("gy")
    me = me_x * n_y + me_y
    devices = n_x * n_y
    rounds = devices // per
    mesh_id = pl.DeviceIdType.MESH

    def place(c, d):
        return (me_x + d) & (n_x - 1), (me_y + (c + d * (n_y // n_x))) & (n_y - 1)

    fetch = pltpu.make_async_copy(hil, order.at[:, pl.ds(0, hil.shape[1])], order_sem)
    fetch.start()
    barrier = pltpu.get_barrier_semaphore()
    for d in range(1, n_y):
        pl.semaphore_signal(barrier, inc=1, device_id=(me_x, (me_y + d) & (n_y - 1)), device_id_type=mesh_id)
    for d in range(1, n_x):
        pl.semaphore_signal(barrier, inc=1, device_id=((me_x + d) & (n_x - 1), me_y), device_id_type=mesh_id)

    for j in range(cap):
        order[0, hil.shape[1] + j] = 0

    def offset(e, total):
        starts[e] = total
        return total + cnt[0, e]

    lax.fori_loop(0, devices, offset, jnp.int32(0), unroll=8)
    fetch.wait()

    def collect(c, slot):
        for d in range(per):
            to_x, to_y = place(c, d)
            start = starts[to_x * n_y + to_y]
            for j in range(cap):
                idx = order[0, start + j]
                rowbuf[slot, d * cap + j : d * cap + j + 1, :] = mixed[pl.ds(idx, 1), :]

    def mlp(c, slot):
        x = rowbuf[slot]
        mlp_in = norm_rows(x, gain[...]).astype(jnp.bfloat16)
        up = jnp.dot(mlp_in, wup[...], preferred_element_type=jnp.float32)
        hidden = jax.nn.gelu(up).astype(jnp.bfloat16)
        y = x + jnp.dot(hidden, wdown[...], preferred_element_type=jnp.float32)
        row = lax.broadcasted_iota(jnp.int32, (cap, C), 0)
        for d in range(per):
            to_x, to_y = place(c, d)
            count = cnt[0, to_x * n_y + to_y]
            send[c * per + d] = jnp.where(row < count, y[d * cap : (d + 1) * cap], 0.0).astype(jnp.bfloat16)

    def copy(c, d):
        i = c * per + d
        return pltpu.make_async_remote_copy(
            src_ref=send.at[i],
            dst_ref=out.at[me],
            send_sem=send_sem.at[i],
            recv_sem=recv_sem.at[i],
            device_id=place(c, d),
            device_id_type=mesh_id,
        )

    collect(0, 0)
    pl.semaphore_wait(barrier, n_x + n_y - 2)
    for d in range(1, n_y):
        pl.semaphore_signal(side_sem, inc=1, device_id=(me_x, (me_y + d) & (n_y - 1)), device_id_type=mesh_id)
    collect(1, 1)
    mlp(0, 0)
    own = pltpu.make_async_copy(send.at[0], out.at[me], own_sem)
    own.start()
    pl.semaphore_wait(side_sem, n_y - 1)
    for d in range(1, per):
        copy(0, d).start()

    def step(k, carry):
        for u in range(2):
            c = 2 * k + 1 + u
            collect(c + 1, u)
            mlp(c, 1 - u)
            for d in range(per):
                copy(c, d).start()
        return carry

    lax.fori_loop(0, rounds // 2 - 1, step, 0)
    mlp(rounds - 1, 1)
    for d in range(per):
        copy(rounds - 1, d).start()
    own.wait()
    for d in range(1, per):
        copy(0, d).wait()

    def finish(c, carry):
        for d in range(per):
            copy(c, d).wait()
        return carry

    lax.fori_loop(1, rounds, finish, 0)


def move_rows(hilbert_order, send_counts, mixed, gain, w_up, w_down, cap):
    devices = send_counts.shape[1]
    rows = hilbert_order.shape[1]
    per = 8
    vm = pl.BlockSpec(memory_space=pltpu.VMEM)
    return pl.pallas_call(
        functools.partial(moved_kernel, cap, per),
        out_shape=jax.ShapeDtypeStruct((devices, cap, C), jnp.bfloat16),
        in_specs=[pl.BlockSpec(memory_space=pl.ANY), pl.BlockSpec(memory_space=pltpu.SMEM)] + [vm] * 4,
        out_specs=pl.BlockSpec(memory_space=pl.ANY),
        scratch_shapes=[
            pltpu.SMEM((1, rows + C), jnp.int32),
            pltpu.SMEM((devices,), jnp.int32),
            pltpu.VMEM((2, per * cap, C), jnp.float32),
            pltpu.VMEM((devices, cap, C), jnp.bfloat16),
            pltpu.SemaphoreType.DMA((devices,)),
            pltpu.SemaphoreType.DMA((devices,)),
            pltpu.SemaphoreType.DMA,
            pltpu.SemaphoreType.DMA,
            pltpu.SemaphoreType.REGULAR,
        ],
        compiler_params=pltpu.CompilerParams(
            vmem_limit_bytes=48 * 2**20, collective_id=1, has_side_effects=True
        ),
        name="move_rows",
    )(hilbert_order, send_counts, mixed, gain, w_up, w_down)


def body(
    points,
    occupied,
    z_order,
    pad_mask,
    hilbert_order,
    send_counts,
    w_conv,
    cpe_proj,
    cpe_gain,
    attn_gain,
    w_qkv,
    w_out,
    mlp_gain,
    w_up,
    w_down,
):
    point_count, width = points.shape
    residual = encode(points, occupied, w_conv, cpe_proj, cpe_gain.reshape(1, width))
    mixed = attention(
        z_order, pad_mask, residual, attn_gain.reshape(1, width), w_qkv, w_out
    )
    device_total = lax.axis_size("gx") * lax.axis_size("gy")
    capacity = point_count // device_total + max(2, point_count // (4 * device_total))
    received = move_rows(
        hilbert_order, send_counts, mixed, mlp_gain.reshape(1, width), w_up, w_down, capacity
    )
    return received.reshape(device_total * capacity, width)


def solution(mesh):
    placed = (
        P(("gx", "gy"), None),
        P(("gx", "gy")),
        P(("gx", "gy"), None),
        P(("gx", "gy"), None),
        P(("gx", "gy"), None),
        P(("gx", "gy"), None),
        P(),
        P(),
        P(),
        P(),
        P(),
        P(),
        P(),
        P(),
        P(),
    )
    return jax.shard_map(
        body, mesh=mesh, in_specs=placed, out_specs=P(("gx", "gy"), None), check_vma=False
    )
```

```python
import functools
import math
import types
import jax
import jax.numpy as jnp
from jax import lax
from jax.experimental import pallas as pl
from jax.experimental.pallas import tpu as pltpu
from jax.sharding import PartitionSpec as P

C = 128
LA = 16
LB = 16
HEADS = 8
PATCH = 1024
HEAD_DIM = 16
QB = 256
UNROLL = 2


def norm_rows(v, gain):
    center = v - jnp.mean(v, axis=-1, keepdims=True)
    spread = jnp.mean(center * center, axis=-1, keepdims=True)
    return center * lax.rsqrt(spread + 1e-05) * gain


LOADS = (
    "pts",
    "occ",
    "order_z",
    "pad",
    "order",
    "cnt",
    "wconv",
    "proj",
    "cgain",
    "again",
    "wqkv",
    "wout",
    "mgain",
    "wup",
    "wdown",
)


def block_kernel(cap, per, names, *refs):
    r = types.SimpleNamespace(**dict(zip(names, refs)))
    rows = r.residual.shape[0]
    loads = {}
    for k, name in enumerate(LOADS):
        source, goal = getattr(r, name + "_in"), getattr(r, name)
        if name == "order":
            goal = goal.at[:, pl.ds(0, rows)]
        loads[name] = pltpu.make_async_copy(source, goal, r.load_sem.at[k])
    for load in loads.values():
        load.start()

    def wait_for(*wanted):
        for name in wanted:
            loads[name].wait()

    encode(r, wait_for)
    attend(r, wait_for)
    move(r, wait_for, cap, per)


def prepare(r):
    qw, vt = r.qw, r.vt
    half = C // 2
    first = lax.broadcasted_iota(jnp.int32, (HEAD_DIM, PATCH), 0) == 0
    unit = jnp.where(first, 1.0, 0.0).astype(jnp.bfloat16)
    for h in range(HEADS):
        qw[h] = jnp.zeros((2 * C, PATCH), jnp.bfloat16)
        qw[h, 3 * half : 3 * half + HEAD_DIM] = unit
        vt[h, HEAD_DIM:] = unit


def encode(r, wait_for):
    pts, occ, wconv, proj, cgain = r.pts, r.occ, r.wconv, r.proj, r.cgain
    residual, win, taps = r.residual, r.win, r.taps
    halo_send, halo_recv, side_sem = r.halo_send, r.halo_recv, r.side_sem
    n_x, n_y = lax.axis_size("gx"), lax.axis_size("gy")
    me_x, me_y = lax.axis_index("gx"), lax.axis_index("gy")
    z = pts.shape[2]
    cols = C // z
    sides = [(dx, dy) for dx in (-1, 0, 1) for dy in (-1, 0, 1) if (dx, dy) != (0, 0)]

    def place(dx, dy):
        return lax.rem(me_x + (dx + n_x), n_x), lax.rem(me_y + (dy + n_y), n_y)

    barrier = pltpu.get_barrier_semaphore()
    row = [((me_x + d) & (n_x - 1), me_y) for d in range(1, n_x)]
    col = [(me_x, (me_y + d) & (n_y - 1)) for d in range(1, n_y)]
    met = row + col + [place(dx, dy) for dx, dy in sides if dx and dy]
    for device in met:
        pl.semaphore_signal(barrier, inc=1, device_id=device, device_id_type=pl.DeviceIdType.MESH)

    rr = lax.broadcasted_iota(jnp.int32, (C, C), 0)
    cc = lax.broadcasted_iota(jnp.int32, (C, C), 1)

    def pick(dz, row):
        hit = (cc == rr + dz) & (rr // z == cc // z)
        return jnp.where(hit, row, 0.0).astype(jnp.bfloat16)

    def put(dz, a, b, block):
        win[dz + 1, a, b] = block.astype(jnp.bfloat16).reshape(block.shape[0] // z, z, C)

    def own_block(r):
        a, b = r // 2, lax.rem(r, 2) * cols
        row = jnp.where(occ[:, pl.ds(pl.multiple_of(r * C, C), C)] > 0, 1.0, 0.0)
        return a, b, row, pts[a, pl.ds(b, cols)].reshape(C, C)

    wait_for("pts", "occ")

    def fill(r, carry):
        a, b, row, block = own_block(r)
        put(0, a + 1, pl.ds(b + 1, cols), jnp.dot(pick(0, row), block, preferred_element_type=jnp.float32))
        return carry

    lax.fori_loop(0, LA * LB // cols, fill, 0, unroll=8)

    def span(d, n):
        here = {-1: pl.ds(1, 1), 0: pl.ds(1, n), 1: pl.ds(n, 1)}[d]
        there = {-1: pl.ds(n + 1, 1), 0: pl.ds(1, n), 1: pl.ds(0, 1)}[d]
        return here, there

    copies = []
    for k, (dx, dy) in enumerate(sides):
        (from_a, to_a), (from_b, to_b) = span(dx, LA), span(dy, LB)
        copies.append(
            pltpu.make_async_remote_copy(
                src_ref=win.at[1, from_a, from_b],
                dst_ref=win.at[1, to_a, to_b],
                send_sem=halo_send.at[k],
                recv_sem=halo_recv.at[k],
                device_id=place(dx, dy),
                device_id_type=pl.DeviceIdType.MESH,
            )
        )
    pl.semaphore_wait(barrier, len(met))
    for copy in copies:
        copy.start()
    for device in col:
        pl.semaphore_signal(side_sem, inc=1, device_id=device, device_id_type=pl.DeviceIdType.MESH)

    def shift(r, carry):
        a, b, row, block = own_block(r)
        for dz in (-1, 1):
            put(dz, a + 1, pl.ds(b + 1, cols), jnp.dot(pick(dz, row), block, preferred_element_type=jnp.float32))
        return carry

    lax.fori_loop(0, LA * LB // cols, shift, 0, unroll=4)
    wait_for("wconv", "proj", "cgain")
    prepare(r)

    none = jnp.zeros((C, C), jnp.bfloat16)
    for i in range(4):
        for sb in range(3):
            for sz in range(3):
                at = ((i * 3 + sb) * 3 + sz) * C
                taps[at : at + C, :C] = wconv[i * 9 + sb * 3 + sz] if i < 3 else none
                taps[at : at + C, C:] = wconv[(i - 1) * 9 + sb * 3 + sz] if i > 0 else none

    for copy in copies:
        copy.wait()

    low_x = jnp.where(me_x > 0, 1.0, 0.0)
    high_x = jnp.where(me_x < n_x - 1, 1.0, 0.0)
    low_y = jnp.where(me_y > 0, 1.0, 0.0)
    high_y = jnp.where(me_y < n_y - 1, 1.0, 0.0)

    def edge(a, b, count, live):
        block = win[1, a, b].reshape(count * z, C)
        for dz in (-1, 0, 1):
            mat = pick(dz, live)[: count * z, : count * z]
            put(dz, a, b, jnp.dot(mat, block, preferred_element_type=jnp.float32))

    for half in range(2):
        run = pl.ds(1 + half * cols, cols)
        edge(0, run, cols, low_x)
        edge(LA + 1, run, cols, high_x)
        edge(run, 0, cols, low_y)
        edge(run, LB + 1, cols, high_y)
    for a, live_x in ((0, low_x), (LA + 1, high_x)):
        for b, live_y in ((0, low_y), (LB + 1, high_y)):
            edge(a, pl.ds(b, 1), 1, live_x * live_y)

    tall = 2
    wide = LB * z

    def conv(t):
        total = None
        for sb in range(3):
            for pair in range(2):
                pieces = []
                for i in (2 * pair, 2 * pair + 1):
                    for sz in range(3):
                        pieces.append(
                            jnp.concatenate(
                                [
                                    win[sz, (t * tall + u) * 2 + i, sb : sb + LB].reshape(wide, C)
                                    for u in range(tall)
                                ],
                                axis=0,
                            )
                        )
                w = jnp.concatenate(
                    [taps[((i * 3 + sb) * 3) * C : ((i * 3 + sb) * 3 + 3) * C, :] for i in (2 * pair, 2 * pair + 1)],
                    axis=0,
                )
                term = jnp.dot(jnp.concatenate(pieces, axis=1), w, preferred_element_type=jnp.float32)
                total = term if total is None else total + term
        for o in range(2):
            conv_out = total[:, o * C : (o + 1) * C].astype(jnp.bfloat16)
            encoded = norm_rows(
                jnp.dot(conv_out, proj[...], preferred_element_type=jnp.float32), cgain[...]
            )
            for u in range(tall):
                a = (t * tall + u) * 2 + o
                residual[a * wide : (a + 1) * wide, :] = (
                    pts[a].reshape(wide, C).astype(jnp.float32) + encoded[u * wide : (u + 1) * wide]
                )

    for t in range(LA // 2 // tall):
        conv(t)


def attend(r, wait_for):
    order_z, pad, again, wqkv, wout = r.order_z, r.pad, r.again, r.wqkv, r.wout
    residual, mixed, serial = r.residual, r.mixed, r.serial
    qw, ka, vt = r.qw, r.ka, r.vt
    heads, live, bd, sbuf = r.heads, r.live, r.bd, r.sbuf
    rows = serial.shape[0]
    blocks = PATCH // QB
    half = C // 2

    def gather(i, carry):
        base = i * 16
        for u in range(16):
            idx = order_z[0, base + u]
            serial[pl.ds(base + u, 1), :] = residual[pl.ds(idx, 1), :]
        return carry

    wait_for("order_z")
    lax.fori_loop(0, rows // 16, gather, 0)
    wait_for("pad", "again", "wqkv", "wout")

    def patch(p, carry):
        off = pl.multiple_of(p * PATCH, PATCH)
        attn_in = norm_rows(serial[pl.ds(off, PATCH), :], again[...]).astype(jnp.bfloat16)
        proj = jnp.dot(attn_in, wqkv[...], preferred_element_type=jnp.float32)
        proj = proj.astype(jnp.bfloat16).astype(jnp.float32)
        qt = proj[:, :C].T * jnp.float32(HEAD_DIM ** -0.5 * math.log2(math.e))
        high = qt.astype(jnp.bfloat16)
        rest = qt - high.astype(jnp.float32)
        mid = rest.astype(jnp.bfloat16)
        low = (rest - mid.astype(jnp.float32)).astype(jnp.bfloat16)
        vals = proj[:, 2 * C :].T.astype(jnp.bfloat16)
        for h in range(HEADS):
            sl = slice(h * HEAD_DIM, (h + 1) * HEAD_DIM)
            at = h % 4 * HEAD_DIM
            qw[h, at : at + HEAD_DIM] = high[sl]
            qw[h, half + at : half + at + HEAD_DIM] = mid[sl]
            qw[h, C + at : C + at + HEAD_DIM] = low[sl]
            vt[h, :HEAD_DIM] = vals[sl]
        rr = lax.broadcasted_iota(jnp.int32, (C, C), 0)
        cc = lax.broadcasted_iota(jnp.int32, (C, C), 1)
        real = jnp.where(pad[:, pl.ds(off, PATCH)] > 0, 1.0, 0.0)
        for b in range(PATCH // C):
            diag = jnp.where(rr == cc, real[:, b * C : (b + 1) * C], 0.0).astype(jnp.bfloat16)
            live[b * C : (b + 1) * C] = jnp.dot(
                diag, jnp.ones((C, C), jnp.bfloat16), preferred_element_type=jnp.float32
            )
        bias = (1.0 - live[...]) * -1e30
        k = proj[:, C : 2 * C]
        kr = pltpu.roll(k, half, 1)
        left = lax.broadcasted_iota(jnp.int32, (PATCH, C), 1) < half
        ka[0, :, :C] = jnp.where(left, k, kr).astype(jnp.bfloat16)
        ka[0, :, C:] = jnp.where(left, k, bias).astype(jnp.bfloat16)
        ka[1, :, :C] = jnp.where(left, kr, k).astype(jnp.bfloat16)
        ka[1, :, C:] = jnp.where(left, kr, bias).astype(jnp.bfloat16)
        rr = lax.broadcasted_iota(jnp.int32, (QB, QB), 0)
        cc = lax.broadcasted_iota(jnp.int32, (QB, QB), 1)
        for b in range(blocks):
            col = bias[b * QB : (b + 1) * QB]
            bd[b] = jnp.where(rr == cc, 0.0, jnp.concatenate([col, col], axis=1))

        def scores(h, b, t):
            g = h // 4
            qs = slice(b * QB, (b + 1) * QB)
            ts = slice(t * QB, (t + 1) * QB)
            if t == b:
                w = jnp.concatenate(
                    [qw[h, : 3 * half, qs], jnp.zeros((half, QB), jnp.bfloat16)], axis=0
                )
                s = jnp.dot(ka[g, ts], w, preferred_element_type=jnp.float32) + bd[b]
            else:
                s = jnp.dot(ka[g, ts], qw[h, :, qs], preferred_element_type=jnp.float32)
            sbuf[b % 2, ts] = s
            return jnp.max(s.reshape(QB // 8, 8, QB), axis=0)

        def values(h, b, t, peak):
            ts = slice(t * QB, (t + 1) * QB)
            prob = jnp.exp2(sbuf[b % 2, ts] - peak).astype(jnp.bfloat16)
            return jnp.dot(vt[h, :, ts], prob, preferred_element_type=jnp.float32)

        def top(parts):
            m = functools.reduce(jnp.maximum, parts)
            return jnp.max(m, axis=0, keepdims=True)

        start = top([scores(0, 0, t) for t in range(blocks)])

        def head(h, peak):
            for b in range(blocks):
                h2, b2 = (h, b + 1) if b + 1 < blocks else (lax.rem(h + 1, HEADS), 0)
                parts = []
                total = None
                for t in range(blocks):
                    parts.append(scores(h2, b2, t))
                    term = values(h, b, t, peak)
                    total = term if total is None else total + term
                heads[pl.ds(pl.multiple_of(h * HEAD_DIM, HEAD_DIM), HEAD_DIM), b * QB : (b + 1) * QB] = (
                    total[:HEAD_DIM] / total[HEAD_DIM : HEAD_DIM + 1]
                )
                peak = top(parts)
            return peak

        lax.fori_loop(0, HEADS, head, start, unroll=UNROLL)
        mixed_heads = heads[...].T.astype(jnp.bfloat16)
        part = jnp.dot(mixed_heads, wout[...], preferred_element_type=jnp.float32)
        at = pl.ds(off, PATCH)
        mixed[at, :] = serial[at, :] + live[...] * part
        return carry

    lax.fori_loop(0, rows // PATCH, patch, 0)


def move(r, wait_for, cap, per):
    out, mixed, order, cnt = r.out, r.mixed, r.order, r.cnt
    mgain, wup, wdown = r.mgain, r.wup, r.wdown
    starts, rowbuf, send = r.starts, r.rowbuf, r.send
    send_sem, recv_sem, own_sem, side_sem = r.send_sem, r.recv_sem, r.own_sem, r.side_sem
    n_x, n_y = lax.axis_size("gx"), lax.axis_size("gy")
    me_x, me_y = lax.axis_index("gx"), lax.axis_index("gy")
    rows = mixed.shape[0]
    me = me_x * n_y + me_y
    devices = n_x * n_y
    rounds = devices // per
    mesh_id = pl.DeviceIdType.MESH

    def target(c, d):
        return (me_x + d) & (n_x - 1), (me_y + (c + d * (n_y // n_x))) & (n_y - 1)

    for j in range(cap):
        order[0, rows + j] = 0

    wait_for("order", "cnt", "mgain", "wup", "wdown")

    def offset(e, total):
        starts[e] = total
        return total + cnt[0, e]

    lax.fori_loop(0, devices, offset, jnp.int32(0), unroll=8)

    def collect(c, slot):
        for d in range(per):
            to_x, to_y = target(c, d)
            start = starts[to_x * n_y + to_y]
            for j in range(cap):
                idx = order[0, start + j]
                rowbuf[slot, d * cap + j : d * cap + j + 1, :] = mixed[pl.ds(idx, 1), :]

    def mlp(c, slot):
        x = rowbuf[slot]
        mlp_in = norm_rows(x, mgain[...]).astype(jnp.bfloat16)
        up = jnp.dot(mlp_in, wup[...], preferred_element_type=jnp.float32)
        hidden = jax.nn.gelu(up).astype(jnp.bfloat16)
        y = x + jnp.dot(hidden, wdown[...], preferred_element_type=jnp.float32)
        row = lax.broadcasted_iota(jnp.int32, (cap, C), 0)
        for d in range(per):
            to_x, to_y = target(c, d)
            count = cnt[0, to_x * n_y + to_y]
            send[c * per + d] = jnp.where(row < count, y[d * cap : (d + 1) * cap], 0.0).astype(jnp.bfloat16)

    def copy(c, d):
        i = c * per + d
        return pltpu.make_async_remote_copy(
            src_ref=send.at[i],
            dst_ref=out.at[me],
            send_sem=send_sem.at[i],
            recv_sem=recv_sem.at[i],
            device_id=target(c, d),
            device_id_type=mesh_id,
        )

    collect(0, 0)
    collect(1, 1)
    mlp(0, 0)
    own = pltpu.make_async_copy(send.at[0], out.at[me], own_sem)
    own.start()
    pl.semaphore_wait(side_sem, n_y - 1)
    for d in range(1, per):
        copy(0, d).start()

    def step(k, carry):
        for u in range(2):
            c = 2 * k + 1 + u
            collect(c + 1, u)
            mlp(c, 1 - u)
            for d in range(per):
                copy(c, d).start()
        return carry

    lax.fori_loop(0, rounds // 2 - 1, step, 0)
    mlp(rounds - 1, 1)
    for d in range(per):
        copy(rounds - 1, d).start()
    own.wait()
    for d in range(1, per):
        copy(0, d).wait()

    def finish(c, carry):
        for d in range(per):
            copy(c, d).wait()
        return carry

    lax.fori_loop(1, rounds, finish, 0)


def body(
    points,
    occupied,
    z_order,
    pad_mask,
    hilbert_order,
    send_counts,
    w_conv,
    cpe_proj,
    cpe_gain,
    attn_gain,
    w_qkv,
    w_out,
    mlp_gain,
    w_up,
    w_down,
):
    rows = points.shape[0]
    depth = rows // (LA * LB)
    devices = lax.axis_size("gx") * lax.axis_size("gy")
    cap = rows // devices + max(2, rows // (4 * devices))
    per = lax.axis_size("gx")
    operands = {
        "pts": points.reshape(LA, LB, depth, C),
        "occ": occupied.reshape(1, rows),
        "order_z": z_order,
        "pad": pad_mask,
        "order": hilbert_order,
        "cnt": send_counts,
        "wconv": w_conv,
        "proj": cpe_proj,
        "cgain": cpe_gain.reshape(1, C),
        "again": attn_gain.reshape(1, C),
        "wqkv": w_qkv,
        "wout": w_out,
        "mgain": mlp_gain.reshape(1, C),
        "wup": w_up,
        "wdown": w_down,
    }
    scratch = {}
    for name, array in operands.items():
        scalar = name in ("order_z", "order", "cnt")
        shape = (1, rows + C) if name == "order" else array.shape
        scratch[name] = (pltpu.SMEM if scalar else pltpu.VMEM)(shape, array.dtype)
    f32, bf16 = jnp.float32, jnp.bfloat16
    dma = pltpu.SemaphoreType.DMA
    scratch.update(
        residual=pltpu.VMEM((rows, C), f32),
        mixed=pltpu.VMEM((rows, C), f32),
        serial=pltpu.VMEM((rows, C), f32),
        win=pltpu.VMEM((3, LA + 2, LB + 2, depth, C), bf16),
        taps=pltpu.VMEM((36 * C, 2 * C), bf16),
        qw=pltpu.VMEM((HEADS, 2 * C, PATCH), bf16),
        ka=pltpu.VMEM((2, PATCH, 2 * C), bf16),
        vt=pltpu.VMEM((HEADS, 2 * HEAD_DIM, PATCH), bf16),
        heads=pltpu.VMEM((C, PATCH), f32),
        live=pltpu.VMEM((PATCH, C), f32),
        bd=pltpu.VMEM((PATCH // QB, QB, QB), f32),
        sbuf=pltpu.VMEM((2, PATCH, QB), f32),
        starts=pltpu.SMEM((devices,), jnp.int32),
        rowbuf=pltpu.VMEM((2, per * cap, C), f32),
        send=pltpu.VMEM((devices, cap, C), bf16),
        load_sem=dma((len(LOADS),)),
        halo_send=dma((8,)),
        halo_recv=dma((8,)),
        send_sem=dma((devices,)),
        recv_sem=dma((devices,)),
        own_sem=dma,
        side_sem=pltpu.SemaphoreType.REGULAR,
    )
    names = [name + "_in" for name in LOADS] + ["out"] + list(scratch)
    moved = pl.pallas_call(
        functools.partial(block_kernel, cap, per, names),
        out_shape=jax.ShapeDtypeStruct((devices, cap, C), bf16),
        in_specs=[pl.BlockSpec(memory_space=pltpu.HBM)] * len(LOADS),
        out_specs=pl.BlockSpec(memory_space=pltpu.HBM),
        scratch_shapes=list(scratch.values()),
        compiler_params=pltpu.CompilerParams(
            vmem_limit_bytes=62 * 2**20, collective_id=0, has_side_effects=True
        ),
        name="block",
    )(*[operands[name] for name in LOADS])
    return moved.reshape(devices * cap, C)


def solution(mesh):
    placed = (
        P(("gx", "gy"), None),
        P(("gx", "gy")),
        P(("gx", "gy"), None),
        P(("gx", "gy"), None),
        P(("gx", "gy"), None),
        P(("gx", "gy"), None),
        P(),
        P(),
        P(),
        P(),
        P(),
        P(),
        P(),
        P(),
        P(),
    )
    return jax.shard_map(
        body, mesh=mesh, in_specs=placed, out_specs=P(("gx", "gy"), None), check_vma=False
    )
```

```python
import functools
import math
import types
import jax
import jax.numpy as jnp
from jax import lax
from jax.experimental import pallas as pl
from jax.experimental.pallas import tpu as pltpu
from jax.sharding import PartitionSpec as P

C = 128
LA = 16
LB = 16
HEADS = 8
PATCH = 1024
HEAD_DIM = 16
QB = 256
KB = 512
UNROLL = 2


def norm_rows(v, gain):
    center = v - jnp.mean(v, axis=-1, keepdims=True)
    spread = jnp.mean(center * center, axis=-1, keepdims=True)
    return center * lax.rsqrt(spread + 1e-05) * gain


LOADS = (
    "pts",
    "occ",
    "order_z",
    "pad",
    "order",
    "cnt",
    "wconv",
    "proj",
    "cgain",
    "again",
    "wqkv",
    "wout",
    "mgain",
    "wup",
    "wdown",
)


def block_kernel(cap, per, names, *refs):
    r = types.SimpleNamespace(**dict(zip(names, refs)))
    rows = r.residual.shape[0]
    loads = {}
    for k, name in enumerate(LOADS):
        source, goal = getattr(r, name + "_in"), getattr(r, name)
        if name == "order":
            goal = goal.at[:, pl.ds(0, rows)]
        loads[name] = pltpu.make_async_copy(source, goal, r.load_sem.at[k])
    for load in loads.values():
        load.start()

    def wait_for(*wanted):
        for name in wanted:
            loads[name].wait()

    encode(r, wait_for)
    attend(r, wait_for)
    move(r, wait_for, cap, per)


def prepare(r):
    qw, vt = r.qw, r.vt
    half = C // 2
    first = lax.broadcasted_iota(jnp.int32, (HEAD_DIM, PATCH), 0) == 0
    unit = jnp.where(first, 1.0, 0.0).astype(jnp.bfloat16)
    for h in range(HEADS):
        qw[h] = jnp.zeros((2 * C, PATCH), jnp.bfloat16)
        qw[h, 3 * half : 3 * half + HEAD_DIM] = unit
        vt[h, HEAD_DIM:] = unit


def offsets(r):
    order, cnt, starts = r.order, r.cnt, r.starts
    rows = order.shape[1] - C
    devices = starts.shape[0]
    for j in range(C):
        order[0, rows + j] = 0

    def offset(e, total):
        starts[e] = total
        return total + cnt[0, e]

    lax.fori_loop(0, devices, offset, jnp.int32(0), unroll=8)


def encode(r, wait_for):
    pts, occ, wconv, proj, cgain = r.pts, r.occ, r.wconv, r.proj, r.cgain
    residual, win, taps = r.residual, r.win, r.taps
    halo_send, halo_recv, side_sem = r.halo_send, r.halo_recv, r.side_sem
    n_x, n_y = lax.axis_size("gx"), lax.axis_size("gy")
    me_x, me_y = lax.axis_index("gx"), lax.axis_index("gy")
    z = pts.shape[2]
    cols = C // z
    sides = [(dx, dy) for dx in (-1, 0, 1) for dy in (-1, 0, 1) if (dx, dy) != (0, 0)]

    def place(dx, dy):
        return lax.rem(me_x + (dx + n_x), n_x), lax.rem(me_y + (dy + n_y), n_y)

    barrier = pltpu.get_barrier_semaphore()
    row = [((me_x + d) & (n_x - 1), me_y) for d in range(1, n_x)]
    col = [(me_x, (me_y + d) & (n_y - 1)) for d in range(1, n_y)]
    met = row + col + [place(dx, dy) for dx, dy in sides if dx and dy]
    for device in met:
        pl.semaphore_signal(barrier, inc=1, device_id=device, device_id_type=pl.DeviceIdType.MESH)

    rr = lax.broadcasted_iota(jnp.int32, (C, C), 0)
    cc = lax.broadcasted_iota(jnp.int32, (C, C), 1)

    def pick(dz, row):
        hit = (cc == rr + dz) & (rr // z == cc // z)
        return jnp.where(hit, row, 0.0).astype(jnp.bfloat16)

    def put(dz, a, b, block):
        win[dz + 1, a, b] = block.astype(jnp.bfloat16).reshape(block.shape[0] // z, z, C)

    def own_block(r):
        a, b = r // 2, lax.rem(r, 2) * cols
        row = jnp.where(occ[:, pl.ds(pl.multiple_of(r * C, C), C)] > 0, 1.0, 0.0)
        return a, b, row, pts[a, pl.ds(b, cols)].reshape(C, C)

    wait_for("pts", "occ")

    def fill(r, carry):
        a, b, row, block = own_block(r)
        put(0, a + 1, pl.ds(b + 1, cols), jnp.dot(pick(0, row), block, preferred_element_type=jnp.float32))
        return carry

    lax.fori_loop(0, LA * LB // cols, fill, 0, unroll=8)

    def span(d, n):
        here = {-1: pl.ds(1, 1), 0: pl.ds(1, n), 1: pl.ds(n, 1)}[d]
        there = {-1: pl.ds(n + 1, 1), 0: pl.ds(1, n), 1: pl.ds(0, 1)}[d]
        return here, there

    copies = []
    for k, (dx, dy) in enumerate(sides):
        (from_a, to_a), (from_b, to_b) = span(dx, LA), span(dy, LB)
        copies.append(
            pltpu.make_async_remote_copy(
                src_ref=win.at[1, from_a, from_b],
                dst_ref=win.at[1, to_a, to_b],
                send_sem=halo_send.at[k],
                recv_sem=halo_recv.at[k],
                device_id=place(dx, dy),
                device_id_type=pl.DeviceIdType.MESH,
            )
        )
    wait_for("order", "cnt")
    offsets(r)
    pl.semaphore_wait(barrier, len(met))
    for copy in copies:
        copy.start()
    for device in col:
        pl.semaphore_signal(side_sem, inc=1, device_id=device, device_id_type=pl.DeviceIdType.MESH)

    def shift(r, carry):
        a, b, row, block = own_block(r)
        for dz in (-1, 1):
            put(dz, a + 1, pl.ds(b + 1, cols), jnp.dot(pick(dz, row), block, preferred_element_type=jnp.float32))
        return carry

    lax.fori_loop(0, LA * LB // cols, shift, 0, unroll=4)
    wait_for("wconv", "proj", "cgain")
    prepare(r)

    none = jnp.zeros((C, C), jnp.bfloat16)
    for i in range(4):
        for sb in range(3):
            for sz in range(3):
                at = ((i * 3 + sb) * 3 + sz) * C
                taps[at : at + C, :C] = wconv[i * 9 + sb * 3 + sz] if i < 3 else none
                taps[at : at + C, C:] = wconv[(i - 1) * 9 + sb * 3 + sz] if i > 0 else none

    for copy in copies:
        copy.wait()

    low_x = jnp.where(me_x > 0, 1.0, 0.0)
    high_x = jnp.where(me_x < n_x - 1, 1.0, 0.0)
    low_y = jnp.where(me_y > 0, 1.0, 0.0)
    high_y = jnp.where(me_y < n_y - 1, 1.0, 0.0)

    def edge(a, b, count, live):
        block = win[1, a, b].reshape(count * z, C)
        for dz in (-1, 0, 1):
            mat = pick(dz, live)[: count * z, : count * z]
            put(dz, a, b, jnp.dot(mat, block, preferred_element_type=jnp.float32))

    for half in range(2):
        run = pl.ds(1 + half * cols, cols)
        edge(0, run, cols, low_x)
        edge(LA + 1, run, cols, high_x)
        edge(run, 0, cols, low_y)
        edge(run, LB + 1, cols, high_y)
    for a, live_x in ((0, low_x), (LA + 1, high_x)):
        for b, live_y in ((0, low_y), (LB + 1, high_y)):
            edge(a, pl.ds(b, 1), 1, live_x * live_y)

    tall = 2
    wide = LB * z

    def conv(t):
        total = None
        for sb in range(3):
            for pair in range(2):
                pieces = []
                for i in (2 * pair, 2 * pair + 1):
                    for sz in range(3):
                        pieces.append(
                            jnp.concatenate(
                                [
                                    win[sz, (t * tall + u) * 2 + i, sb : sb + LB].reshape(wide, C)
                                    for u in range(tall)
                                ],
                                axis=0,
                            )
                        )
                w = jnp.concatenate(
                    [taps[((i * 3 + sb) * 3) * C : ((i * 3 + sb) * 3 + 3) * C, :] for i in (2 * pair, 2 * pair + 1)],
                    axis=0,
                )
                term = jnp.dot(jnp.concatenate(pieces, axis=1), w, preferred_element_type=jnp.float32)
                total = term if total is None else total + term
        for o in range(2):
            conv_out = total[:, o * C : (o + 1) * C].astype(jnp.bfloat16)
            encoded = norm_rows(
                jnp.dot(conv_out, proj[...], preferred_element_type=jnp.float32), cgain[...]
            )
            for u in range(tall):
                a = (t * tall + u) * 2 + o
                residual[a * wide : (a + 1) * wide, :] = (
                    pts[a].reshape(wide, C).astype(jnp.float32) + encoded[u * wide : (u + 1) * wide]
                )

    for t in range(LA // 2 // tall):
        conv(t)


def attend(r, wait_for):
    order_z, pad, again, wqkv, wout = r.order_z, r.pad, r.again, r.wqkv, r.wout
    residual, mixed, serial = r.residual, r.mixed, r.serial
    qw, ka, vt = r.qw, r.ka, r.vt
    heads, live, own, sbuf = r.heads, r.live, r.own, r.sbuf
    rows = serial.shape[0]
    blocks = PATCH // QB
    half = C // 2

    def gather(base, count):
        for u in range(count):
            idx = order_z[0, base + u]
            serial[pl.ds(base + u, 1), :] = residual[pl.ds(idx, 1), :]

    def gather_some(i, carry):
        gather(i * 16, 16)
        return carry

    wait_for("order_z")
    lax.fori_loop(0, PATCH // 16, gather_some, 0)
    wait_for("pad", "again", "wqkv", "wout")

    def patch(p, carry):
        off = pl.multiple_of(p * PATCH, PATCH)
        attn_in = norm_rows(serial[pl.ds(off, PATCH), :], again[...]).astype(jnp.bfloat16)
        proj = jnp.dot(attn_in, wqkv[...], preferred_element_type=jnp.float32)
        proj = proj.astype(jnp.bfloat16)
        turned = proj.T
        qt = turned[:C].astype(jnp.float32) * jnp.float32(HEAD_DIM ** -0.5 * math.log2(math.e))
        high = qt.astype(jnp.bfloat16)
        rest = qt - high.astype(jnp.float32)
        mid = rest.astype(jnp.bfloat16)
        low = (rest - mid.astype(jnp.float32)).astype(jnp.bfloat16)
        vals = turned[2 * C :]
        for h in range(HEADS):
            sl = slice(h * HEAD_DIM, (h + 1) * HEAD_DIM)
            at = h % 4 * HEAD_DIM
            qw[h, at : at + HEAD_DIM] = high[sl]
            qw[h, half + at : half + at + HEAD_DIM] = mid[sl]
            qw[h, C + at : C + at + HEAD_DIM] = low[sl]
            vt[h, :HEAD_DIM] = vals[sl]
        rr = lax.broadcasted_iota(jnp.int32, (C, C), 0)
        cc = lax.broadcasted_iota(jnp.int32, (C, C), 1)
        real = jnp.where(pad[:, pl.ds(off, PATCH)] > 0, 1.0, 0.0)
        for b in range(PATCH // C):
            diag = jnp.where(rr == cc, real[:, b * C : (b + 1) * C], 0.0).astype(jnp.bfloat16)
            live[b * C : (b + 1) * C] = jnp.dot(
                diag, jnp.ones((C, C), jnp.bfloat16), preferred_element_type=jnp.float32
            )
        bias = (1.0 - live[...]) * -1e30
        k = proj[:, C : 2 * C].astype(jnp.float32)
        kr = pltpu.roll(k, half, 1)
        left = lax.broadcasted_iota(jnp.int32, (PATCH, C), 1) < half
        ka[0, :, :C] = jnp.where(left, k, kr).astype(jnp.bfloat16)
        ka[0, :, C:] = jnp.where(left, k, bias).astype(jnp.bfloat16)
        ka[1, :, :C] = jnp.where(left, kr, k).astype(jnp.bfloat16)
        ka[1, :, C:] = jnp.where(left, kr, bias).astype(jnp.bfloat16)
        keyed = qt * turned[C : 2 * C].astype(jnp.float32)
        own[...] = jnp.sum(keyed.reshape(HEADS, HEAD_DIM, PATCH), axis=1, keepdims=True)
        rr = lax.broadcasted_iota(jnp.int32, (QB, QB), 0)
        cc = lax.broadcasted_iota(jnp.int32, (QB, QB), 1)

        def scores(h, b, t):
            qs = slice(b * QB, (b + 1) * QB)
            s = jnp.dot(
                ka[h // 4, t * KB : (t + 1) * KB], qw[h, :, qs], preferred_element_type=jnp.float32
            )
            pieces = [s[i * QB : (i + 1) * QB] for i in range(KB // QB)]
            same = b - t * (KB // QB)
            if 0 <= same < len(pieces):
                pieces[same] = jnp.where(rr == cc, own[h, :, qs], pieces[same])
            tops = []
            for i, piece in enumerate(pieces):
                sbuf[b % 2, t * KB + i * QB : t * KB + (i + 1) * QB] = piece
                tops.append(jnp.max(piece.reshape(QB // 8, 8, QB), axis=0))
            return functools.reduce(jnp.maximum, tops)

        def values(h, b, t, peak):
            ts = slice(t * KB, (t + 1) * KB)
            prob = jnp.exp2(sbuf[b % 2, ts] - peak).astype(jnp.bfloat16)
            return jnp.dot(vt[h, :, ts], prob, preferred_element_type=jnp.float32)

        def top(parts):
            m = functools.reduce(jnp.maximum, parts)
            return jnp.max(m, axis=0, keepdims=True)

        start = top([scores(0, 0, t) for t in range(PATCH // KB)])

        def head(h, peak):
            share = PATCH // HEADS
            gather(pl.multiple_of(lax.rem(p + 1, rows // PATCH) * PATCH + h * share, share), share)
            for b in range(blocks):
                h2, b2 = (h, b + 1) if b + 1 < blocks else (lax.rem(h + 1, HEADS), 0)
                parts = []
                total = None
                for t in range(PATCH // KB):
                    parts.append(scores(h2, b2, t))
                    term = values(h, b, t, peak)
                    total = term if total is None else total + term
                heads[pl.ds(pl.multiple_of(h * HEAD_DIM, HEAD_DIM), HEAD_DIM), b * QB : (b + 1) * QB] = (
                    total[:HEAD_DIM] / total[HEAD_DIM : HEAD_DIM + 1]
                )
                peak = top(parts)
            return peak

        lax.fori_loop(0, HEADS, head, start, unroll=UNROLL)
        mixed_heads = heads[...].astype(jnp.bfloat16).T
        part = jnp.dot(mixed_heads, wout[...], preferred_element_type=jnp.float32)
        at = pl.ds(off, PATCH)
        mixed[at, :] = serial[at, :] + live[...] * part
        return carry

    lax.fori_loop(0, rows // PATCH, patch, 0)


def move(r, wait_for, cap, per):
    out, mixed, order, cnt = r.out, r.mixed, r.order, r.cnt
    mgain, wup, wdown = r.mgain, r.wup, r.wdown
    starts, rowbuf, send = r.starts, r.rowbuf, r.send
    send_sem, recv_sem, own_sem, side_sem = r.send_sem, r.recv_sem, r.own_sem, r.side_sem
    n_x, n_y = lax.axis_size("gx"), lax.axis_size("gy")
    me_x, me_y = lax.axis_index("gx"), lax.axis_index("gy")
    rows = mixed.shape[0]
    me = me_x * n_y + me_y
    devices = n_x * n_y
    rounds = devices // per
    mesh_id = pl.DeviceIdType.MESH

    def target(c, d):
        return me_x ^ d, me_y ^ (c ^ (d * (n_y // n_x)))

    wait_for("mgain", "wup", "wdown")

    def collect(c, slot):
        for d in range(per):
            to_x, to_y = target(c, d)
            start = starts[to_x * n_y + to_y]
            for j in range(cap):
                idx = order[0, start + j]
                rowbuf[slot, d * cap + j : d * cap + j + 1, :] = mixed[pl.ds(idx, 1), :]

    def mlp(c, slot):
        x = rowbuf[slot]
        mlp_in = norm_rows(x, mgain[...]).astype(jnp.bfloat16)
        up = jnp.dot(mlp_in, wup[...], preferred_element_type=jnp.float32)
        hidden = jax.nn.gelu(up).astype(jnp.bfloat16)
        y = x + jnp.dot(hidden, wdown[...], preferred_element_type=jnp.float32)
        row = lax.broadcasted_iota(jnp.int32, (cap, C), 0)
        for d in range(per):
            to_x, to_y = target(c, d)
            count = cnt[0, to_x * n_y + to_y]
            send[c * per + d] = jnp.where(row < count, y[d * cap : (d + 1) * cap], 0.0).astype(jnp.bfloat16)

    def copy(c, d):
        i = c * per + d
        return pltpu.make_async_remote_copy(
            src_ref=send.at[i],
            dst_ref=out.at[me],
            send_sem=send_sem.at[i],
            recv_sem=recv_sem.at[i],
            device_id=target(c, d),
            device_id_type=mesh_id,
        )

    collect(0, 0)
    mlp(0, 0)
    own = pltpu.make_async_copy(send.at[0], out.at[me], own_sem)
    own.start()
    pl.semaphore_wait(side_sem, n_y - 1)
    for d in range(1, per):
        copy(0, d).start()
    collect(1, 1)

    def step(k, carry):
        for u in range(2):
            c = 2 * k + 1 + u
            collect(c + 1, u)
            mlp(c, 1 - u)
            for d in range(per):
                copy(c, d).start()
        return carry

    lax.fori_loop(0, rounds // 2 - 1, step, 0)
    mlp(rounds - 1, 1)
    for d in range(per):
        copy(rounds - 1, d).start()
    own.wait()
    for d in range(1, per):
        copy(0, d).wait()

    def finish(c, carry):
        for d in range(per):
            copy(c, d).wait()
        return carry

    lax.fori_loop(1, rounds, finish, 0)


def body(
    points,
    occupied,
    z_order,
    pad_mask,
    hilbert_order,
    send_counts,
    w_conv,
    cpe_proj,
    cpe_gain,
    attn_gain,
    w_qkv,
    w_out,
    mlp_gain,
    w_up,
    w_down,
):
    rows = points.shape[0]
    depth = rows // (LA * LB)
    devices = lax.axis_size("gx") * lax.axis_size("gy")
    cap = rows // devices + max(2, rows // (4 * devices))
    per = lax.axis_size("gx")
    operands = {
        "pts": points.reshape(LA, LB, depth, C),
        "occ": occupied.reshape(1, rows),
        "order_z": z_order,
        "pad": pad_mask,
        "order": hilbert_order,
        "cnt": send_counts,
        "wconv": w_conv,
        "proj": cpe_proj,
        "cgain": cpe_gain.reshape(1, C),
        "again": attn_gain.reshape(1, C),
        "wqkv": w_qkv,
        "wout": w_out,
        "mgain": mlp_gain.reshape(1, C),
        "wup": w_up,
        "wdown": w_down,
    }
    scratch = {}
    for name, array in operands.items():
        scalar = name in ("order_z", "order", "cnt")
        shape = (1, rows + C) if name == "order" else array.shape
        scratch[name] = (pltpu.SMEM if scalar else pltpu.VMEM)(shape, array.dtype)
    f32, bf16 = jnp.float32, jnp.bfloat16
    dma = pltpu.SemaphoreType.DMA
    scratch.update(
        residual=pltpu.VMEM((rows, C), f32),
        mixed=pltpu.VMEM((rows, C), f32),
        serial=pltpu.VMEM((rows, C), f32),
        win=pltpu.VMEM((3, LA + 2, LB + 2, depth, C), bf16),
        taps=pltpu.VMEM((36 * C, 2 * C), bf16),
        qw=pltpu.VMEM((HEADS, 2 * C, PATCH), bf16),
        ka=pltpu.VMEM((2, PATCH, 2 * C), bf16),
        vt=pltpu.VMEM((HEADS, 2 * HEAD_DIM, PATCH), bf16),
        heads=pltpu.VMEM((C, PATCH), f32),
        live=pltpu.VMEM((PATCH, C), f32),
        own=pltpu.VMEM((HEADS, 1, PATCH), f32),
        sbuf=pltpu.VMEM((2, PATCH, QB), f32),
        starts=pltpu.SMEM((devices,), jnp.int32),
        rowbuf=pltpu.VMEM((2, per * cap, C), f32),
        send=pltpu.VMEM((devices, cap, C), bf16),
        load_sem=dma((len(LOADS),)),
        halo_send=dma((8,)),
        halo_recv=dma((8,)),
        send_sem=dma((devices,)),
        recv_sem=dma((devices,)),
        own_sem=dma,
        side_sem=pltpu.SemaphoreType.REGULAR,
    )
    names = [name + "_in" for name in LOADS] + ["out"] + list(scratch)
    moved = pl.pallas_call(
        functools.partial(block_kernel, cap, per, names),
        out_shape=jax.ShapeDtypeStruct((devices, cap, C), bf16),
        in_specs=[pl.BlockSpec(memory_space=pltpu.HBM)] * len(LOADS),
        out_specs=pl.BlockSpec(memory_space=pltpu.HBM),
        scratch_shapes=list(scratch.values()),
        compiler_params=pltpu.CompilerParams(
            vmem_limit_bytes=62 * 2**20, collective_id=0, has_side_effects=True
        ),
        name="block",
    )(*[operands[name] for name in LOADS])
    return moved.reshape(devices * cap, C)


def solution(mesh):
    placed = (
        P(("gx", "gy"), None),
        P(("gx", "gy")),
        P(("gx", "gy"), None),
        P(("gx", "gy"), None),
        P(("gx", "gy"), None),
        P(("gx", "gy"), None),
        P(),
        P(),
        P(),
        P(),
        P(),
        P(),
        P(),
        P(),
        P(),
    )
    return jax.shard_map(
        body, mesh=mesh, in_specs=placed, out_specs=P(("gx", "gy"), None), check_vma=False
    )
```

```python
import functools
import math
import types
import jax
import jax.numpy as jnp
from jax import lax
from jax.experimental import pallas as pl
from jax.experimental.pallas import tpu as pltpu
from jax.sharding import PartitionSpec as P

C = 128
LA = 16
LB = 16
HEADS = 8
PATCH = 1024
HEAD_DIM = 16
QB = 256
KB = 512
UNROLL = 2


def norm_rows(v, gain):
    center = v - jnp.mean(v, axis=-1, keepdims=True)
    spread = jnp.mean(center * center, axis=-1, keepdims=True)
    return center * lax.rsqrt(spread + 1e-05) * gain


LOADS = (
    "pts",
    "occ",
    "order_z",
    "pad",
    "order",
    "cnt",
    "wconv",
    "proj",
    "cgain",
    "again",
    "wqkv",
    "wout",
    "mgain",
    "wup",
    "wdown",
)


def block_kernel(cap, per, names, *refs):
    r = types.SimpleNamespace(**dict(zip(names, refs)))
    rows = r.residual.shape[0]
    loads = {}
    for k, name in enumerate(LOADS):
        source, goal = getattr(r, name + "_in"), getattr(r, name)
        if name == "order":
            goal = goal.at[:, pl.ds(0, rows)]
        loads[name] = pltpu.make_async_copy(source, goal, r.load_sem.at[k])
    for load in loads.values():
        load.start()

    def wait_for(*wanted):
        for name in wanted:
            loads[name].wait()

    encode(r, wait_for)
    attend(r, wait_for)
    move(r, wait_for, cap, per)


def prepare(r):
    qw, vt = r.qw, r.vt
    half = C // 2
    first = lax.broadcasted_iota(jnp.int32, (HEAD_DIM, PATCH), 0) == 0
    unit = jnp.where(first, 1.0, 0.0).astype(jnp.bfloat16)
    for h in range(HEADS):
        qw[h] = jnp.zeros((2 * C, PATCH), jnp.bfloat16)
        qw[h, 3 * half : 3 * half + HEAD_DIM] = unit
        vt[h, HEAD_DIM:] = unit


def offsets(r):
    order, cnt, starts = r.order, r.cnt, r.starts
    rows = order.shape[1] - C
    devices = starts.shape[0]
    for j in range(C):
        order[0, rows + j] = 0

    def offset(e, total):
        starts[e] = total
        return total + cnt[0, e]

    lax.fori_loop(0, devices, offset, jnp.int32(0), unroll=8)


def encode(r, wait_for):
    pts, occ, wconv, proj, cgain = r.pts, r.occ, r.wconv, r.proj, r.cgain
    residual, win, taps, early = r.residual, r.win, r.taps, r.early
    halo_send, halo_recv, side_sem = r.halo_send, r.halo_recv, r.side_sem
    n_x, n_y = lax.axis_size("gx"), lax.axis_size("gy")
    me_x, me_y = lax.axis_index("gx"), lax.axis_index("gy")
    z = pts.shape[2]
    cols = C // z
    sides = [(dx, dy) for dx in (-1, 0, 1) for dy in (-1, 0, 1) if (dx, dy) != (0, 0)]

    def place(dx, dy):
        return lax.rem(me_x + (dx + n_x), n_x), lax.rem(me_y + (dy + n_y), n_y)

    barrier = pltpu.get_barrier_semaphore()
    row = [((me_x + d) & (n_x - 1), me_y) for d in range(1, n_x)]
    col = [(me_x, (me_y + d) & (n_y - 1)) for d in range(1, n_y)]
    met = row + col + [place(dx, dy) for dx, dy in sides if dx and dy]
    for device in met:
        pl.semaphore_signal(barrier, inc=1, device_id=device, device_id_type=pl.DeviceIdType.MESH)

    rr = lax.broadcasted_iota(jnp.int32, (C, C), 0)
    cc = lax.broadcasted_iota(jnp.int32, (C, C), 1)

    def pick(dz, row):
        hit = (cc == rr + dz) & (rr // z == cc // z)
        return jnp.where(hit, row, 0.0).astype(jnp.bfloat16)

    def put(dz, a, b, block):
        win[dz + 1, a, b] = block.astype(jnp.bfloat16).reshape(block.shape[0] // z, z, C)

    def own_block(r):
        a, b = r // 2, lax.rem(r, 2) * cols
        row = jnp.where(occ[:, pl.ds(pl.multiple_of(r * C, C), C)] > 0, 1.0, 0.0)
        return a, b, row, pts[a, pl.ds(b, cols)].reshape(C, C)

    wait_for("pts", "occ")

    def fill(r, carry):
        a, b, row, block = own_block(r)
        put(0, a + 1, pl.ds(b + 1, cols), jnp.dot(pick(0, row), block, preferred_element_type=jnp.float32))
        return carry

    lax.fori_loop(0, LA * LB // cols, fill, 0, unroll=8)

    def span(d, n):
        here = {-1: pl.ds(1, 1), 0: pl.ds(1, n), 1: pl.ds(n, 1)}[d]
        there = {-1: pl.ds(n + 1, 1), 0: pl.ds(1, n), 1: pl.ds(0, 1)}[d]
        return here, there

    copies = []
    for k, (dx, dy) in enumerate(sides):
        (from_a, to_a), (from_b, to_b) = span(dx, LA), span(dy, LB)
        copies.append(
            pltpu.make_async_remote_copy(
                src_ref=win.at[1, from_a, from_b],
                dst_ref=win.at[1, to_a, to_b],
                send_sem=halo_send.at[k],
                recv_sem=halo_recv.at[k],
                device_id=place(dx, dy),
                device_id_type=pl.DeviceIdType.MESH,
            )
        )

    def shift(r, carry):
        a, b, row, block = own_block(r)
        for dz in (-1, 1):
            put(dz, a + 1, pl.ds(b + 1, cols), jnp.dot(pick(dz, row), block, preferred_element_type=jnp.float32))
        return carry

    lax.fori_loop(0, LA * LB // cols, shift, 0, unroll=4)
    wait_for("order", "cnt")
    offsets(r)
    pl.semaphore_wait(barrier, len(met))
    for copy in copies:
        copy.start()
    for device in col:
        pl.semaphore_signal(side_sem, inc=1, device_id=device, device_id_type=pl.DeviceIdType.MESH)

    wait_for("wconv", "proj", "cgain")
    prepare(r)

    none = jnp.zeros((C, C), jnp.bfloat16)
    for i in range(4):
        for sb in range(3):
            for sz in range(3):
                at = ((i * 3 + sb) * 3 + sz) * C
                taps[at : at + C, :C] = wconv[i * 9 + sb * 3 + sz] if i < 3 else none
                taps[at : at + C, C:] = wconv[(i - 1) * 9 + sb * 3 + sz] if i > 0 else none

    tall = 2
    wide = LB * z
    inner = range(1, LA // 2 // tall - 1)

    def products(t, sb):
        total = None
        for pair in range(2):
            pieces = []
            for i in (2 * pair, 2 * pair + 1):
                for sz in range(3):
                    pieces.append(
                        jnp.concatenate(
                            [
                                win[sz, (t * tall + u) * 2 + i, sb : sb + LB].reshape(wide, C)
                                for u in range(tall)
                            ],
                            axis=0,
                        )
                    )
            w = jnp.concatenate(
                [taps[((i * 3 + sb) * 3) * C : ((i * 3 + sb) * 3 + 3) * C, :] for i in (2 * pair, 2 * pair + 1)],
                axis=0,
            )
            term = jnp.dot(jnp.concatenate(pieces, axis=1), w, preferred_element_type=jnp.float32)
            total = term if total is None else total + term
        return total

    for t in inner:
        early[t - 1] = products(t, 1)
    for copy in copies:
        copy.wait()

    low_x = jnp.where(me_x > 0, 1.0, 0.0)
    high_x = jnp.where(me_x < n_x - 1, 1.0, 0.0)
    low_y = jnp.where(me_y > 0, 1.0, 0.0)
    high_y = jnp.where(me_y < n_y - 1, 1.0, 0.0)

    def edge(a, b, count, live):
        block = win[1, a, b].reshape(count * z, C)
        for dz in (-1, 0, 1):
            mat = pick(dz, live)[: count * z, : count * z]
            put(dz, a, b, jnp.dot(mat, block, preferred_element_type=jnp.float32))

    for half in range(2):
        run = pl.ds(1 + half * cols, cols)
        edge(0, run, cols, low_x)
        edge(LA + 1, run, cols, high_x)
        edge(run, 0, cols, low_y)
        edge(run, LB + 1, cols, high_y)
    for a, live_x in ((0, low_x), (LA + 1, high_x)):
        for b, live_y in ((0, low_y), (LB + 1, high_y)):
            edge(a, pl.ds(b, 1), 1, live_x * live_y)

    def conv(t):
        total = early[t - 1] if t in inner else products(t, 1)
        total = total + products(t, 0)
        total = total + products(t, 2)
        for o in range(2):
            conv_out = total[:, o * C : (o + 1) * C].astype(jnp.bfloat16)
            encoded = norm_rows(
                jnp.dot(conv_out, proj[...], preferred_element_type=jnp.float32), cgain[...]
            )
            for u in range(tall):
                a = (t * tall + u) * 2 + o
                residual[a * wide : (a + 1) * wide, :] = (
                    pts[a].reshape(wide, C).astype(jnp.float32) + encoded[u * wide : (u + 1) * wide]
                )

    for t in range(LA // 2 // tall):
        conv(t)


def attend(r, wait_for):
    order_z, pad, again, wqkv, wout = r.order_z, r.pad, r.again, r.wqkv, r.wout
    residual, mixed, serial = r.residual, r.mixed, r.serial
    qw, ka, vt = r.qw, r.ka, r.vt
    heads, live, own, sbuf = r.heads, r.live, r.own, r.sbuf
    rows = serial.shape[0]
    blocks = PATCH // QB
    half = C // 2

    def gather(base, count):
        for u in range(count):
            idx = order_z[0, base + u]
            serial[pl.ds(base + u, 1), :] = residual[pl.ds(idx, 1), :]

    def gather_some(i, carry):
        gather(i * 16, 16)
        return carry

    wait_for("order_z")
    lax.fori_loop(0, PATCH // 16, gather_some, 0)
    wait_for("pad", "again", "wqkv", "wout")

    def patch(p, carry):
        off = pl.multiple_of(p * PATCH, PATCH)
        attn_in = norm_rows(serial[pl.ds(off, PATCH), :], again[...]).astype(jnp.bfloat16)
        proj = jnp.dot(attn_in, wqkv[...], preferred_element_type=jnp.float32)
        proj = proj.astype(jnp.bfloat16)
        turned = proj.T
        qt = turned[:C].astype(jnp.float32) * jnp.float32(HEAD_DIM ** -0.5 * math.log2(math.e))
        high = qt.astype(jnp.bfloat16)
        rest = qt - high.astype(jnp.float32)
        mid = rest.astype(jnp.bfloat16)
        low = (rest - mid.astype(jnp.float32)).astype(jnp.bfloat16)
        vals = turned[2 * C :]
        for h in range(HEADS):
            sl = slice(h * HEAD_DIM, (h + 1) * HEAD_DIM)
            at = h % 4 * HEAD_DIM
            qw[h, at : at + HEAD_DIM] = high[sl]
            qw[h, half + at : half + at + HEAD_DIM] = mid[sl]
            qw[h, C + at : C + at + HEAD_DIM] = low[sl]
            vt[h, :HEAD_DIM] = vals[sl]
        rr = lax.broadcasted_iota(jnp.int32, (C, C), 0)
        cc = lax.broadcasted_iota(jnp.int32, (C, C), 1)
        real = jnp.where(pad[:, pl.ds(off, PATCH)] > 0, 1.0, 0.0)
        for b in range(PATCH // C):
            diag = jnp.where(rr == cc, real[:, b * C : (b + 1) * C], 0.0).astype(jnp.bfloat16)
            live[b * C : (b + 1) * C] = jnp.dot(
                diag, jnp.ones((C, C), jnp.bfloat16), preferred_element_type=jnp.float32
            )
        bias = (1.0 - live[...]) * -1e30
        k = proj[:, C : 2 * C].astype(jnp.float32)
        kr = pltpu.roll(k, half, 1)
        left = lax.broadcasted_iota(jnp.int32, (PATCH, C), 1) < half
        ka[0, :, :C] = jnp.where(left, k, kr).astype(jnp.bfloat16)
        ka[0, :, C:] = jnp.where(left, k, bias).astype(jnp.bfloat16)
        ka[1, :, :C] = jnp.where(left, kr, k).astype(jnp.bfloat16)
        ka[1, :, C:] = jnp.where(left, kr, bias).astype(jnp.bfloat16)
        keyed = qt * turned[C : 2 * C].astype(jnp.float32)
        own[...] = jnp.sum(keyed.reshape(HEADS, HEAD_DIM, PATCH), axis=1, keepdims=True)
        rr = lax.broadcasted_iota(jnp.int32, (QB, QB), 0)
        cc = lax.broadcasted_iota(jnp.int32, (QB, QB), 1)

        def scores(h, b, t):
            qs = slice(b * QB, (b + 1) * QB)
            s = jnp.dot(
                ka[h // 4, t * KB : (t + 1) * KB], qw[h, :, qs], preferred_element_type=jnp.float32
            )
            pieces = [s[i * QB : (i + 1) * QB] for i in range(KB // QB)]
            same = b - t * (KB // QB)
            if 0 <= same < len(pieces):
                pieces[same] = jnp.where(rr == cc, own[h, :, qs], pieces[same])
            tops = []
            for i, piece in enumerate(pieces):
                sbuf[b % 2, t * KB + i * QB : t * KB + (i + 1) * QB] = piece
                tops.append(jnp.max(piece.reshape(QB // 8, 8, QB), axis=0))
            return functools.reduce(jnp.maximum, tops)

        def values(h, b, t, peak):
            ts = slice(t * KB, (t + 1) * KB)
            prob = jnp.exp2(sbuf[b % 2, ts] - peak).astype(jnp.bfloat16)
            return jnp.dot(vt[h, :, ts], prob, preferred_element_type=jnp.float32)

        def top(parts):
            m = functools.reduce(jnp.maximum, parts)
            return jnp.max(m, axis=0, keepdims=True)

        start = top([scores(0, 0, t) for t in range(PATCH // KB)])

        def head(h, peak):
            share = PATCH // HEADS
            gather(pl.multiple_of(lax.rem(p + 1, rows // PATCH) * PATCH + h * share, share), share)
            for b in range(blocks):
                h2, b2 = (h, b + 1) if b + 1 < blocks else (lax.rem(h + 1, HEADS), 0)
                parts = []
                total = None
                for t in range(PATCH // KB):
                    parts.append(scores(h2, b2, t))
                    term = values(h, b, t, peak)
                    total = term if total is None else total + term
                heads[pl.ds(pl.multiple_of(h * HEAD_DIM, HEAD_DIM), HEAD_DIM), b * QB : (b + 1) * QB] = (
                    total[:HEAD_DIM] / total[HEAD_DIM : HEAD_DIM + 1]
                )
                peak = top(parts)
            return peak

        lax.fori_loop(0, HEADS, head, start, unroll=UNROLL)
        mixed_heads = heads[...].astype(jnp.bfloat16).T
        part = jnp.dot(mixed_heads, wout[...], preferred_element_type=jnp.float32)
        at = pl.ds(off, PATCH)
        mixed[at, :] = serial[at, :] + live[...] * part
        return carry

    lax.fori_loop(0, rows // PATCH, patch, 0)


def move(r, wait_for, cap, per):
    out, mixed, order, cnt = r.out, r.mixed, r.order, r.cnt
    mgain, wup, wdown = r.mgain, r.wup, r.wdown
    starts, rowbuf, send = r.starts, r.rowbuf, r.send
    send_sem, recv_sem, own_sem, side_sem = r.send_sem, r.recv_sem, r.own_sem, r.side_sem
    n_x, n_y = lax.axis_size("gx"), lax.axis_size("gy")
    me_x, me_y = lax.axis_index("gx"), lax.axis_index("gy")
    rows = mixed.shape[0]
    me = me_x * n_y + me_y
    devices = n_x * n_y
    rounds = devices // per
    mesh_id = pl.DeviceIdType.MESH

    def target(c, d):
        return (me_x + d) & (n_x - 1), me_y ^ (c ^ (d * (n_y // n_x)))

    wait_for("mgain", "wup", "wdown")

    def collect(c, slot):
        for d in range(per):
            to_x, to_y = target(c, d)
            start = starts[to_x * n_y + to_y]
            for j in range(cap):
                idx = order[0, start + j]
                rowbuf[slot, d * cap + j : d * cap + j + 1, :] = mixed[pl.ds(idx, 1), :]

    def mlp(c, slot):
        x = rowbuf[slot]
        mlp_in = norm_rows(x, mgain[...]).astype(jnp.bfloat16)
        up = jnp.dot(mlp_in, wup[...], preferred_element_type=jnp.float32)
        hidden = jax.nn.gelu(up).astype(jnp.bfloat16)
        y = x + jnp.dot(hidden, wdown[...], preferred_element_type=jnp.float32)
        row = lax.broadcasted_iota(jnp.int32, (cap, C), 0)
        for d in range(per):
            to_x, to_y = target(c, d)
            count = cnt[0, to_x * n_y + to_y]
            send[c * per + d] = jnp.where(row < count, y[d * cap : (d + 1) * cap], 0.0).astype(jnp.bfloat16)

    def copy(c, d):
        i = c * per + d
        return pltpu.make_async_remote_copy(
            src_ref=send.at[i],
            dst_ref=out.at[me],
            send_sem=send_sem.at[i],
            recv_sem=recv_sem.at[i],
            device_id=target(c, d),
            device_id_type=mesh_id,
        )

    collect(0, 0)
    mlp(0, 0)
    own = pltpu.make_async_copy(send.at[0], out.at[me], own_sem)
    own.start()
    pl.semaphore_wait(side_sem, n_y - 1)
    for d in range(1, per):
        copy(0, d).start()
    collect(1, 1)

    def step(k, carry):
        for u in range(2):
            c = 2 * k + 1 + u
            collect(c + 1, u)
            mlp(c, 1 - u)
            for d in range(per):
                copy(c, d).start()
        return carry

    lax.fori_loop(0, rounds // 2 - 1, step, 0)
    mlp(rounds - 1, 1)
    for d in range(per):
        copy(rounds - 1, d).start()
    own.wait()
    for d in range(1, per):
        copy(0, d).wait()

    def finish(c, carry):
        for d in range(per):
            copy(c, d).wait()
        return carry

    lax.fori_loop(1, rounds, finish, 0)


def body(
    points,
    occupied,
    z_order,
    pad_mask,
    hilbert_order,
    send_counts,
    w_conv,
    cpe_proj,
    cpe_gain,
    attn_gain,
    w_qkv,
    w_out,
    mlp_gain,
    w_up,
    w_down,
):
    rows = points.shape[0]
    depth = rows // (LA * LB)
    devices = lax.axis_size("gx") * lax.axis_size("gy")
    cap = rows // devices + max(2, rows // (4 * devices))
    per = lax.axis_size("gx")
    operands = {
        "pts": points.reshape(LA, LB, depth, C),
        "occ": occupied.reshape(1, rows),
        "order_z": z_order,
        "pad": pad_mask,
        "order": hilbert_order,
        "cnt": send_counts,
        "wconv": w_conv,
        "proj": cpe_proj,
        "cgain": cpe_gain.reshape(1, C),
        "again": attn_gain.reshape(1, C),
        "wqkv": w_qkv,
        "wout": w_out,
        "mgain": mlp_gain.reshape(1, C),
        "wup": w_up,
        "wdown": w_down,
    }
    scratch = {}
    for name, array in operands.items():
        scalar = name in ("order_z", "order", "cnt")
        shape = (1, rows + C) if name == "order" else array.shape
        scratch[name] = (pltpu.SMEM if scalar else pltpu.VMEM)(shape, array.dtype)
    f32, bf16 = jnp.float32, jnp.bfloat16
    dma = pltpu.SemaphoreType.DMA
    scratch.update(
        residual=pltpu.VMEM((rows, C), f32),
        mixed=pltpu.VMEM((rows, C), f32),
        serial=pltpu.VMEM((rows, C), f32),
        win=pltpu.VMEM((3, LA + 2, LB + 2, depth, C), bf16),
        taps=pltpu.VMEM((36 * C, 2 * C), bf16),
        early=pltpu.VMEM((LA // 4 - 2, 2 * LB * depth, 2 * C), f32),
        qw=pltpu.VMEM((HEADS, 2 * C, PATCH), bf16),
        ka=pltpu.VMEM((2, PATCH, 2 * C), bf16),
        vt=pltpu.VMEM((HEADS, 2 * HEAD_DIM, PATCH), bf16),
        heads=pltpu.VMEM((C, PATCH), f32),
        live=pltpu.VMEM((PATCH, C), f32),
        own=pltpu.VMEM((HEADS, 1, PATCH), f32),
        sbuf=pltpu.VMEM((2, PATCH, QB), f32),
        starts=pltpu.SMEM((devices,), jnp.int32),
        rowbuf=pltpu.VMEM((2, per * cap, C), f32),
        send=pltpu.VMEM((devices, cap, C), bf16),
        load_sem=dma((len(LOADS),)),
        halo_send=dma((8,)),
        halo_recv=dma((8,)),
        send_sem=dma((devices,)),
        recv_sem=dma((devices,)),
        own_sem=dma,
        side_sem=pltpu.SemaphoreType.REGULAR,
    )
    names = [name + "_in" for name in LOADS] + ["out"] + list(scratch)
    moved = pl.pallas_call(
        functools.partial(block_kernel, cap, per, names),
        out_shape=jax.ShapeDtypeStruct((devices, cap, C), bf16),
        in_specs=[pl.BlockSpec(memory_space=pltpu.HBM)] * len(LOADS),
        out_specs=pl.BlockSpec(memory_space=pltpu.HBM),
        scratch_shapes=list(scratch.values()),
        compiler_params=pltpu.CompilerParams(
            vmem_limit_bytes=62 * 2**20, collective_id=0, has_side_effects=True
        ),
        name="block",
    )(*[operands[name] for name in LOADS])
    return moved.reshape(devices * cap, C)


def solution(mesh):
    placed = (
        P(("gx", "gy"), None),
        P(("gx", "gy")),
        P(("gx", "gy"), None),
        P(("gx", "gy"), None),
        P(("gx", "gy"), None),
        P(("gx", "gy"), None),
        P(),
        P(),
        P(),
        P(),
        P(),
        P(),
        P(),
        P(),
        P(),
    )
    return jax.shard_map(
        body, mesh=mesh, in_specs=placed, out_specs=P(("gx", "gy"), None), check_vma=False
    )
```

```python
import functools
import math
import types
import jax
import jax.numpy as jnp
from jax import lax
from jax.experimental import pallas as pl
from jax.experimental.pallas import tpu as pltpu
from jax.sharding import PartitionSpec as P

C = 128
LA = 16
LB = 16
HEADS = 8
PATCH = 1024
HEAD_DIM = 16
QB = 256
KB = 512
UNROLL = 4


def norm_rows(v, gain):
    center = v - jnp.mean(v, axis=-1, keepdims=True)
    spread = jnp.mean(center * center, axis=-1, keepdims=True)
    return center * lax.rsqrt(spread + 1e-05) * gain


LOADS = (
    "pts",
    "occ",
    "order_z",
    "pad",
    "order",
    "cnt",
    "wconv",
    "proj",
    "cgain",
    "again",
    "wqkv",
    "wout",
    "mgain",
    "wup",
    "wdown",
)


def block_kernel(cap, per, names, *refs):
    r = types.SimpleNamespace(**dict(zip(names, refs)))
    rows = r.residual.shape[0]
    loads = {}
    for k, name in enumerate(LOADS):
        source, goal = getattr(r, name + "_in"), getattr(r, name)
        if name == "order":
            goal = goal.at[:, pl.ds(0, rows)]
        loads[name] = pltpu.make_async_copy(source, goal, r.load_sem.at[k])
    for load in loads.values():
        load.start()

    def wait_for(*wanted):
        for name in wanted:
            loads[name].wait()

    encode(r, wait_for)
    attend(r, wait_for)
    move(r, wait_for, cap, per)


def prepare(r):
    qw, vt = r.qw, r.vt
    half = C // 2
    first = lax.broadcasted_iota(jnp.int32, (HEAD_DIM, PATCH), 0) == 0
    unit = jnp.where(first, 1.0, 0.0).astype(jnp.bfloat16)
    for h in range(HEADS):
        qw[h] = jnp.zeros((2 * C, PATCH), jnp.bfloat16)
        qw[h, 3 * half : 3 * half + HEAD_DIM] = unit
        vt[h, HEAD_DIM:] = unit


def offsets(r):
    order, cnt, starts = r.order, r.cnt, r.starts
    rows = order.shape[1] - C
    devices = starts.shape[0]
    for j in range(C):
        order[0, rows + j] = 0

    def offset(e, total):
        starts[e] = total
        return total + cnt[0, e]

    lax.fori_loop(0, devices, offset, jnp.int32(0), unroll=8)


def encode(r, wait_for):
    pts, occ, wconv, proj, cgain = r.pts, r.occ, r.wconv, r.proj, r.cgain
    residual, win, taps, early = r.residual, r.win, r.taps, r.early
    halo_send, halo_recv, side_sem = r.halo_send, r.halo_recv, r.side_sem
    n_x, n_y = lax.axis_size("gx"), lax.axis_size("gy")
    me_x, me_y = lax.axis_index("gx"), lax.axis_index("gy")
    z = pts.shape[2]
    cols = C // z
    sides = [(dx, dy) for dx in (-1, 0, 1) for dy in (-1, 0, 1) if (dx, dy) != (0, 0)]

    def place(dx, dy):
        return lax.rem(me_x + (dx + n_x), n_x), lax.rem(me_y + (dy + n_y), n_y)

    barrier = pltpu.get_barrier_semaphore()
    row = [((me_x + d) & (n_x - 1), me_y) for d in range(1, n_x)]
    col = [(me_x, (me_y + d) & (n_y - 1)) for d in range(1, n_y)]
    met = row + col + [place(dx, dy) for dx, dy in sides if dx and dy]
    for device in met:
        pl.semaphore_signal(barrier, inc=1, device_id=device, device_id_type=pl.DeviceIdType.MESH)

    rr = lax.broadcasted_iota(jnp.int32, (C, C), 0)
    cc = lax.broadcasted_iota(jnp.int32, (C, C), 1)

    def pick(dz, row):
        hit = (cc == rr + dz) & (rr // z == cc // z)
        return jnp.where(hit, row, 0.0).astype(jnp.bfloat16)

    def put(dz, a, b, block):
        win[dz + 1, a, b] = block.astype(jnp.bfloat16).reshape(block.shape[0] // z, z, C)

    def own_block(r):
        a, b = r // 2, lax.rem(r, 2) * cols
        row = jnp.where(occ[:, pl.ds(pl.multiple_of(r * C, C), C)] > 0, 1.0, 0.0)
        return a, b, row, pts[a, pl.ds(b, cols)].reshape(C, C)

    wait_for("pts", "occ")

    def fill(r, carry):
        a, b, row, block = own_block(r)
        put(0, a + 1, pl.ds(b + 1, cols), jnp.dot(pick(0, row), block, preferred_element_type=jnp.float32))
        return carry

    lax.fori_loop(0, LA * LB // cols, fill, 0, unroll=8)

    def span(d, n):
        here = {-1: pl.ds(1, 1), 0: pl.ds(1, n), 1: pl.ds(n, 1)}[d]
        there = {-1: pl.ds(n + 1, 1), 0: pl.ds(1, n), 1: pl.ds(0, 1)}[d]
        return here, there

    copies = []
    for k, (dx, dy) in enumerate(sides):
        (from_a, to_a), (from_b, to_b) = span(dx, LA), span(dy, LB)
        copies.append(
            pltpu.make_async_remote_copy(
                src_ref=win.at[1, from_a, from_b],
                dst_ref=win.at[1, to_a, to_b],
                send_sem=halo_send.at[k],
                recv_sem=halo_recv.at[k],
                device_id=place(dx, dy),
                device_id_type=pl.DeviceIdType.MESH,
            )
        )

    def shift(r, carry):
        a, b, row, block = own_block(r)
        for dz in (-1, 1):
            put(dz, a + 1, pl.ds(b + 1, cols), jnp.dot(pick(dz, row), block, preferred_element_type=jnp.float32))
        return carry

    lax.fori_loop(0, LA * LB // cols, shift, 0, unroll=4)
    wait_for("order", "cnt")
    offsets(r)
    pl.semaphore_wait(barrier, len(met))
    for copy in copies:
        copy.start()
    for device in col:
        pl.semaphore_signal(side_sem, inc=1, device_id=device, device_id_type=pl.DeviceIdType.MESH)

    wait_for("wconv", "proj", "cgain")
    prepare(r)

    none = jnp.zeros((C, C), jnp.bfloat16)
    for i in range(4):
        for sb in range(3):
            for sz in range(3):
                at = ((i * 3 + sb) * 3 + sz) * C
                taps[at : at + C, :C] = wconv[i * 9 + sb * 3 + sz] if i < 3 else none
                taps[at : at + C, C:] = wconv[(i - 1) * 9 + sb * 3 + sz] if i > 0 else none

    tall = 2
    wide = LB * z
    steps = LA // 2 // tall
    edges = {0: (1,), steps - 1: (0,)}

    def products(t, sb, pairs=(0, 1)):
        total = None
        for pair in pairs:
            pieces = []
            for i in (2 * pair, 2 * pair + 1):
                for sz in range(3):
                    pieces.append(
                        jnp.concatenate(
                            [
                                win[sz, (t * tall + u) * 2 + i, sb : sb + LB].reshape(wide, C)
                                for u in range(tall)
                            ],
                            axis=0,
                        )
                    )
            w = jnp.concatenate(
                [taps[((i * 3 + sb) * 3) * C : ((i * 3 + sb) * 3 + 3) * C, :] for i in (2 * pair, 2 * pair + 1)],
                axis=0,
            )
            term = jnp.dot(jnp.concatenate(pieces, axis=1), w, preferred_element_type=jnp.float32)
            total = term if total is None else total + term
        return total

    for t in range(steps):
        early[t] = products(t, 1, edges.get(t, (0, 1)))
    for copy in copies:
        copy.wait()

    low_x = jnp.where(me_x > 0, 1.0, 0.0)
    high_x = jnp.where(me_x < n_x - 1, 1.0, 0.0)
    low_y = jnp.where(me_y > 0, 1.0, 0.0)
    high_y = jnp.where(me_y < n_y - 1, 1.0, 0.0)

    def edge(a, b, count, live):
        block = win[1, a, b].reshape(count * z, C)
        for dz in (-1, 0, 1):
            mat = pick(dz, live)[: count * z, : count * z]
            put(dz, a, b, jnp.dot(mat, block, preferred_element_type=jnp.float32))

    for half in range(2):
        run = pl.ds(1 + half * cols, cols)
        edge(0, run, cols, low_x)
        edge(LA + 1, run, cols, high_x)
        edge(run, 0, cols, low_y)
        edge(run, LB + 1, cols, high_y)
    for a, live_x in ((0, low_x), (LA + 1, high_x)):
        for b, live_y in ((0, low_y), (LB + 1, high_y)):
            edge(a, pl.ds(b, 1), 1, live_x * live_y)

    def conv(t):
        total = early[t] + products(t, 0)
        if t in edges:
            total = total + products(t, 1, (1 - edges[t][0],))
        total = total + products(t, 2)
        for o in range(2):
            conv_out = total[:, o * C : (o + 1) * C].astype(jnp.bfloat16)
            encoded = norm_rows(
                jnp.dot(conv_out, proj[...], preferred_element_type=jnp.float32), cgain[...]
            )
            for u in range(tall):
                a = (t * tall + u) * 2 + o
                residual[a * wide : (a + 1) * wide, :] = (
                    pts[a].reshape(wide, C).astype(jnp.float32) + encoded[u * wide : (u + 1) * wide]
                )

    for t in range(steps):
        conv(t)


def attend(r, wait_for):
    order_z, pad, again, wqkv, wout = r.order_z, r.pad, r.again, r.wqkv, r.wout
    residual, mixed, serial = r.residual, r.mixed, r.serial
    qw, ka, vt = r.qw, r.ka, r.vt
    heads, live, own, sbuf = r.heads, r.live, r.own, r.sbuf
    rows = serial.shape[0]
    blocks = PATCH // QB
    half = C // 2

    def gather(base, count):
        for u in range(count):
            idx = order_z[0, base + u]
            serial[pl.ds(base + u, 1), :] = residual[pl.ds(idx, 1), :]

    def gather_some(i, carry):
        gather(i * 16, 16)
        return carry

    wait_for("order_z")
    lax.fori_loop(0, PATCH // 16, gather_some, 0)
    wait_for("pad", "again", "wqkv", "wout")

    def patch(p, carry):
        off = pl.multiple_of(p * PATCH, PATCH)
        attn_in = norm_rows(serial[pl.ds(off, PATCH), :], again[...]).astype(jnp.bfloat16)
        proj = jnp.dot(attn_in, wqkv[...], preferred_element_type=jnp.float32)
        proj = proj.astype(jnp.bfloat16)
        turned = proj.T
        qt = turned[:C].astype(jnp.float32) * jnp.float32(HEAD_DIM ** -0.5 * math.log2(math.e))
        high = qt.astype(jnp.bfloat16)
        rest = qt - high.astype(jnp.float32)
        mid = rest.astype(jnp.bfloat16)
        low = (rest - mid.astype(jnp.float32)).astype(jnp.bfloat16)
        vals = turned[2 * C :]
        for h in range(HEADS):
            sl = slice(h * HEAD_DIM, (h + 1) * HEAD_DIM)
            at = h % 4 * HEAD_DIM
            qw[h, at : at + HEAD_DIM] = high[sl]
            qw[h, half + at : half + at + HEAD_DIM] = mid[sl]
            qw[h, C + at : C + at + HEAD_DIM] = low[sl]
            vt[h, :HEAD_DIM] = vals[sl]
        rr = lax.broadcasted_iota(jnp.int32, (C, C), 0)
        cc = lax.broadcasted_iota(jnp.int32, (C, C), 1)
        real = jnp.where(pad[:, pl.ds(off, PATCH)] > 0, 1.0, 0.0)
        for b in range(PATCH // C):
            diag = jnp.where(rr == cc, real[:, b * C : (b + 1) * C], 0.0).astype(jnp.bfloat16)
            live[b * C : (b + 1) * C] = jnp.dot(
                diag, jnp.ones((C, C), jnp.bfloat16), preferred_element_type=jnp.float32
            )
        bias = (1.0 - live[...]) * -1e30
        k = proj[:, C : 2 * C].astype(jnp.float32)
        kr = pltpu.roll(k, half, 1)
        left = lax.broadcasted_iota(jnp.int32, (PATCH, C), 1) < half
        ka[0, :, :C] = jnp.where(left, k, kr).astype(jnp.bfloat16)
        ka[0, :, C:] = jnp.where(left, k, bias).astype(jnp.bfloat16)
        ka[1, :, :C] = jnp.where(left, kr, k).astype(jnp.bfloat16)
        ka[1, :, C:] = jnp.where(left, kr, bias).astype(jnp.bfloat16)
        keyed = qt * turned[C : 2 * C].astype(jnp.float32)
        own[...] = jnp.sum(keyed.reshape(HEADS, HEAD_DIM, PATCH), axis=1, keepdims=True)
        rr = lax.broadcasted_iota(jnp.int32, (QB, QB), 0)
        cc = lax.broadcasted_iota(jnp.int32, (QB, QB), 1)

        def scores(h, b, t):
            qs = slice(b * QB, (b + 1) * QB)
            s = jnp.dot(
                ka[h // 4, t * KB : (t + 1) * KB], qw[h, :, qs], preferred_element_type=jnp.float32
            )
            pieces = [s[i * QB : (i + 1) * QB] for i in range(KB // QB)]
            same = b - t * (KB // QB)
            if 0 <= same < len(pieces):
                pieces[same] = jnp.where(rr == cc, own[h, :, qs], pieces[same])
            tops = []
            for i, piece in enumerate(pieces):
                sbuf[b % 2, t * KB + i * QB : t * KB + (i + 1) * QB] = piece
                tops.append(jnp.max(piece.reshape(QB // 8, 8, QB), axis=0))
            return functools.reduce(jnp.maximum, tops)

        def values(h, b, t, peak):
            ts = slice(t * KB, (t + 1) * KB)
            prob = jnp.exp2(sbuf[b % 2, ts] - peak).astype(jnp.bfloat16)
            return jnp.dot(vt[h, :, ts], prob, preferred_element_type=jnp.float32)

        def top(parts):
            m = functools.reduce(jnp.maximum, parts)
            return jnp.max(m, axis=0, keepdims=True)

        start = top([scores(0, 0, t) for t in range(PATCH // KB)])

        def head(h, peak):
            share = PATCH // HEADS
            gather(pl.multiple_of(lax.rem(p + 1, rows // PATCH) * PATCH + h * share, share), share)
            for b in range(blocks):
                h2, b2 = (h, b + 1) if b + 1 < blocks else (lax.rem(h + 1, HEADS), 0)
                parts = []
                total = None
                for t in range(PATCH // KB):
                    parts.append(scores(h2, b2, t))
                    term = values(h, b, t, peak)
                    total = term if total is None else total + term
                heads[pl.ds(pl.multiple_of(h * HEAD_DIM, HEAD_DIM), HEAD_DIM), b * QB : (b + 1) * QB] = (
                    total[:HEAD_DIM] / total[HEAD_DIM : HEAD_DIM + 1]
                )
                peak = top(parts)
            return peak

        lax.fori_loop(0, HEADS, head, start, unroll=UNROLL)
        mixed_heads = heads[...].astype(jnp.bfloat16).T
        part = jnp.dot(mixed_heads, wout[...], preferred_element_type=jnp.float32)
        at = pl.ds(off, PATCH)
        mixed[at, :] = serial[at, :] + live[...] * part
        return carry

    lax.fori_loop(0, rows // PATCH, patch, 0)


def move(r, wait_for, cap, per):
    out, mixed, order, cnt = r.out, r.mixed, r.order, r.cnt
    mgain, wup, wdown = r.mgain, r.wup, r.wdown
    starts, rowbuf, send = r.starts, r.rowbuf, r.send
    send_sem, recv_sem, own_sem, side_sem = r.send_sem, r.recv_sem, r.own_sem, r.side_sem
    n_x, n_y = lax.axis_size("gx"), lax.axis_size("gy")
    me_x, me_y = lax.axis_index("gx"), lax.axis_index("gy")
    rows = mixed.shape[0]
    me = me_x * n_y + me_y
    devices = n_x * n_y
    rounds = devices // per
    mesh_id = pl.DeviceIdType.MESH

    def target(c, d):
        return (me_x + d) & (n_x - 1), me_y ^ (c ^ (d * (n_y // n_x)))

    wait_for("mgain", "wup", "wdown")

    def collect(c, slot):
        for d in range(per):
            to_x, to_y = target(c, d)
            start = starts[to_x * n_y + to_y]
            for j in range(cap):
                idx = order[0, start + j]
                rowbuf[slot, d * cap + j : d * cap + j + 1, :] = mixed[pl.ds(idx, 1), :]

    def mlp(c, slot):
        x = rowbuf[slot]
        mlp_in = norm_rows(x, mgain[...]).astype(jnp.bfloat16)
        up = jnp.dot(mlp_in, wup[...], preferred_element_type=jnp.float32)
        hidden = jax.nn.gelu(up).astype(jnp.bfloat16)
        y = x + jnp.dot(hidden, wdown[...], preferred_element_type=jnp.float32)
        row = lax.broadcasted_iota(jnp.int32, (cap, C), 0)
        for d in range(per):
            to_x, to_y = target(c, d)
            count = cnt[0, to_x * n_y + to_y]
            send[c * per + d] = jnp.where(row < count, y[d * cap : (d + 1) * cap], 0.0).astype(jnp.bfloat16)

    def copy(c, d):
        i = c * per + d
        return pltpu.make_async_remote_copy(
            src_ref=send.at[i],
            dst_ref=out.at[me],
            send_sem=send_sem.at[i],
            recv_sem=recv_sem.at[i],
            device_id=target(c, d),
            device_id_type=mesh_id,
        )

    collect(0, 0)
    mlp(0, 0)
    own = pltpu.make_async_copy(send.at[0], out.at[me], own_sem)
    own.start()
    pl.semaphore_wait(side_sem, n_y - 1)
    for d in range(1, per):
        copy(0, d).start()
    collect(1, 1)

    def step(k, carry):
        for u in range(2):
            c = 2 * k + 1 + u
            collect(c + 1, u)
            mlp(c, 1 - u)
            for d in range(per):
                copy(c, d).start()
        return carry

    lax.fori_loop(0, rounds // 2 - 1, step, 0)
    mlp(rounds - 1, 1)
    for d in range(per):
        copy(rounds - 1, d).start()
    own.wait()
    for d in range(1, per):
        copy(0, d).wait()

    def finish(c, carry):
        for d in range(per):
            copy(c, d).wait()
        return carry

    lax.fori_loop(1, rounds, finish, 0)


def body(
    points,
    occupied,
    z_order,
    pad_mask,
    hilbert_order,
    send_counts,
    w_conv,
    cpe_proj,
    cpe_gain,
    attn_gain,
    w_qkv,
    w_out,
    mlp_gain,
    w_up,
    w_down,
):
    rows = points.shape[0]
    depth = rows // (LA * LB)
    devices = lax.axis_size("gx") * lax.axis_size("gy")
    cap = rows // devices + max(2, rows // (4 * devices))
    per = lax.axis_size("gx")
    operands = {
        "pts": points.reshape(LA, LB, depth, C),
        "occ": occupied.reshape(1, rows),
        "order_z": z_order,
        "pad": pad_mask,
        "order": hilbert_order,
        "cnt": send_counts,
        "wconv": w_conv,
        "proj": cpe_proj,
        "cgain": cpe_gain.reshape(1, C),
        "again": attn_gain.reshape(1, C),
        "wqkv": w_qkv,
        "wout": w_out,
        "mgain": mlp_gain.reshape(1, C),
        "wup": w_up,
        "wdown": w_down,
    }
    scratch = {}
    for name, array in operands.items():
        scalar = name in ("order_z", "order", "cnt")
        shape = (1, rows + C) if name == "order" else array.shape
        scratch[name] = (pltpu.SMEM if scalar else pltpu.VMEM)(shape, array.dtype)
    f32, bf16 = jnp.float32, jnp.bfloat16
    dma = pltpu.SemaphoreType.DMA
    scratch.update(
        residual=pltpu.VMEM((rows, C), f32),
        mixed=pltpu.VMEM((rows, C), f32),
        serial=pltpu.VMEM((rows, C), f32),
        win=pltpu.VMEM((3, LA + 2, LB + 2, depth, C), bf16),
        taps=pltpu.VMEM((36 * C, 2 * C), bf16),
        early=pltpu.VMEM((LA // 4, 2 * LB * depth, 2 * C), f32),
        qw=pltpu.VMEM((HEADS, 2 * C, PATCH), bf16),
        ka=pltpu.VMEM((2, PATCH, 2 * C), bf16),
        vt=pltpu.VMEM((HEADS, 2 * HEAD_DIM, PATCH), bf16),
        heads=pltpu.VMEM((C, PATCH), f32),
        live=pltpu.VMEM((PATCH, C), f32),
        own=pltpu.VMEM((HEADS, 1, PATCH), f32),
        sbuf=pltpu.VMEM((2, PATCH, QB), f32),
        starts=pltpu.SMEM((devices,), jnp.int32),
        rowbuf=pltpu.VMEM((2, per * cap, C), f32),
        send=pltpu.VMEM((devices, cap, C), bf16),
        load_sem=dma((len(LOADS),)),
        halo_send=dma((8,)),
        halo_recv=dma((8,)),
        send_sem=dma((devices,)),
        recv_sem=dma((devices,)),
        own_sem=dma,
        side_sem=pltpu.SemaphoreType.REGULAR,
    )
    names = [name + "_in" for name in LOADS] + ["out"] + list(scratch)
    moved = pl.pallas_call(
        functools.partial(block_kernel, cap, per, names),
        out_shape=jax.ShapeDtypeStruct((devices, cap, C), bf16),
        in_specs=[pl.BlockSpec(memory_space=pltpu.HBM)] * len(LOADS),
        out_specs=pl.BlockSpec(memory_space=pltpu.HBM),
        scratch_shapes=list(scratch.values()),
        compiler_params=pltpu.CompilerParams(
            vmem_limit_bytes=62 * 2**20, collective_id=0, has_side_effects=True
        ),
        name="block",
    )(*[operands[name] for name in LOADS])
    return moved.reshape(devices * cap, C)


def solution(mesh):
    placed = (
        P(("gx", "gy"), None),
        P(("gx", "gy")),
        P(("gx", "gy"), None),
        P(("gx", "gy"), None),
        P(("gx", "gy"), None),
        P(("gx", "gy"), None),
        P(),
        P(),
        P(),
        P(),
        P(),
        P(),
        P(),
        P(),
        P(),
    )
    return jax.shard_map(
        body, mesh=mesh, in_specs=placed, out_specs=P(("gx", "gy"), None), check_vma=False
    )
```
